32 devices in a mesh: groups: 2 (over y), branch: 2 (over core), dap: 4 (over z), tile: 2 (over x).
Axes of the slice: x: 2, y: 2, z: 4, core: 2. Of those that a mesh axis runs over, the one named last changes fastest.
Arguments:
- homolog_hidden: bfloat16 [64, 256, 256], P(('groups', 'dap'), ('branch', 'tile')), parts along dimension 0, may hold values from -6 to 6
- duo_hidden: bfloat16 [512, 256, 128], P(('groups', 'branch', 'tile'), 'dap'), parts along dimension 0, may hold values from -6 to 6
- homolog_valid_flags: int32 [64, 256], P(('groups', 'dap'), ('branch', 'tile')), parts along dimension 0, may hold values 0 or 1
- duo_valid_flags: int32 [512, 256], P(('groups', 'branch', 'tile'), 'dap'), parts along dimension 0, may hold values 0 or 1
- polymer_labeling: int32 [512], P('groups'), parts along dimension 0, may hold values from 0 to 3, never falling along the last dimension, each value on 1 to 128 neighbouring positions
- monomer_serials: int32 [512], P('groups'), parts along dimension 0, may hold values from 0 to 510, as said below
- separation_bin_vectors: bfloat16 [66, 128], replicated, may hold values from -4 to 4
- duo_logit_rescale: float32 [128], replicated, may hold values from 0.25 to 1.75
- duo_logit_projector: bfloat16 [128, 8], replicated, may hold values from -0.5 to 0.5
- homolog_heeded_rescale: float32 [256], replicated, may hold values from 0.25 to 1.75
- qkv_valve_projectors: bfloat16 [256, 1024], replicated
- heeded_exit_projector: bfloat16 [256, 256], replicated, may hold values from -0.375 to 0.375
- dyadic_rescale: float32 [256], replicated, may hold values from 0.25 to 1.75
- dyadic_factor_projector: bfloat16 [256, 64], replicated, may hold values from -0.375 to 0.375
- dyadic_exit_projector: bfloat16 [1024, 128], replicated, may hold values from -1.5 to 1.5
- triad_entry_rescales: float32 [2, 128], replicated, may hold values from 0.25 to 1.75
- triad_entry_projectors: bfloat16 [2, 128, 512], replicated, may hold values from -0.5 to 0.5
- triad_valve_projectors: bfloat16 [2, 128, 128], replicated, may hold values from -0.5 to 0.5
- triad_exit_rescales: float32 [2, 128], replicated, may hold values from 0.25 to 1.75
- triad_exit_projectors: bfloat16 [2, 128, 128], replicated, may hold values from -0.5 to 0.5
Outputs:
- lineup_updated_state: bfloat16 [64, 256, 256], P(('groups', 'dap'), ('branch', 'tile')), parts along dimension 0
- pair_out: bfloat16 [512, 256, 128], P(('groups', 'branch', 'tile'), 'dap'), parts along dimension 0
The draws below stay inside these ranges and needn't reach their ends.
There are 2 independent parts, one for each index of `groups`. The reference program is written for one: setup_inputs(seed, part) draws one part's arguments, and reference() takes and returns one part's arrays. A program takes and returns all parts, laid end to end along the dimension named above; an argument that names none is the same for every part. Nothing has to cross between parts.
Inputs may be any that keep to these rules, and one draw needn't show every extreme that they name: `monomer_serials`: starts at 0 and rises by 1 to 3 from each residue to the next. `polymer_labeling`: chains are contiguous runs of 1 to 128 residues, numbered in order.
All inputs are finite; a program needn't handle non-finite values. No bound on the sum of `homolog_valid_flags` or of `duo_valid_flags` on one device may be relied on, other than what follows from the above.
Results may differ from the reference program's by a relative error of at most 0.015.
Values may be sent and summed in bfloat16 or wider, within the bound.
A program may use at most 128 MiB of HBM per device.

```python
import math
import jax
import jax.numpy as jnp
import numpy as np
from jax import lax

ALIGN_FEATURES = 256
DUAL_DIM = 128
FOCUS_GROUPS = 8
GROUP_CHANNEL = 32
TENSORED_FEATS = 32
TRIAD_DIM = 128
REL_BINS = 66
CUT_AMINO_SITES = 256
ALIGN_STRANDS = 32


def draw_homolog_hidden(key, part):
    seed_stochastic_token = jax.random.normal(key, (ALIGN_STRANDS, CUT_AMINO_SITES, ALIGN_FEATURES), jnp.float32)
    return jnp.clip(seed_stochastic_token, -6.0, 6.0).astype(jnp.bfloat16)


def draw_qkv_valve_projectors(key, part):
    seed_stochastic_token = jax.random.normal(key, (ALIGN_FEATURES, 4 * ALIGN_FEATURES), jnp.float32) * ALIGN_FEATURES ** (-0.5)
    return seed_stochastic_token.astype(jnp.bfloat16)


def draw_monomer_serials(key, part):
    half_count = CUT_AMINO_SITES // 2
    first_steps = jax.random.randint(key, (half_count,), 1, 4, dtype=jnp.int32)
    last_pair = jnp.arange(half_count, dtype=jnp.int32) == half_count - 1
    first_steps = jnp.where(last_pair, jnp.int32(2), first_steps).astype(jnp.int32)
    step_sizes = jnp.stack([first_steps, 4 - first_steps], axis=1).reshape(CUT_AMINO_SITES).astype(jnp.int32)
    running = jnp.cumsum(step_sizes).astype(jnp.int32)
    return jnp.concatenate([jnp.zeros((1,), jnp.int32), running[:-1]]).astype(jnp.int32)


def plant(array, own_key, low, largest):
    dims = array.shape
    spot = [jax.random.randint(jax.random.fold_in(own_key, axis), (), 0, dims[axis]) for axis in range(len(dims))]
    array = array.at[tuple(spot)].set(low)
    longest = dims.index(max(dims))
    spot[longest] = (spot[longest] + 1) % dims[longest]
    return array.at[tuple(spot)].set(largest)


def steps_of(own_key, extent, split, smallest, top_value):
    def one(dim, parts):
        draws = jax.random.uniform(jax.random.fold_in(jax.random.fold_in(own_key, 6), dim), (parts,), jnp.float32, smallest / len(split), top_value / len(split))
        return jnp.repeat(jnp.exp(draws), extent[dim] // parts).reshape((-1,) + (1,) * (len(extent) - dim - 1))

    loudness = one(*split[0])
    for cut in split[1:]:
        loudness = loudness * one(*cut)
    return loudness


def length_profile(number_of, total, reach, slope):
    weights = [(1 << 20) // math.isqrt(standing ** slope) + 1 for standing in range(2, number_of + 1)]
    surplus, given = total - reach - (number_of - 1), [1] * (number_of - 1)
    while surplus > 0:
        candidates = [i for i in range(number_of - 1) if given[i] < reach]
        mass, budget = sum([weights[i] for i in candidates]), surplus
        for i in candidates:
            more = min(reach - given[i], max(1, budget * weights[i] // mass), surplus)
            given[i] = given[i] + more
            surplus = surplus - more
    return np.array([reach] + given)


def uneven_parts(rng, number_of, total, reach, slope):
    if number_of == 2:
        one = jax.random.randint(rng, (), max(1, total - reach), min(reach, total - 1) + 1)
        return jnp.stack([one, total - one])
    tallies = jnp.asarray(length_profile(number_of, total, reach, slope), jnp.int32)
    couples = (number_of - 1) // 2
    donor, sink = tallies[1:1 + 2 * couples:2], tallies[2:2 + 2 * couples:2]
    slack = jnp.minimum(donor - 1, reach - sink)
    passed = jax.random.randint(jax.random.fold_in(rng, 1), (couples,), 0, 1 << 20) % (slack + 1)
    tallies = tallies.at[1:1 + 2 * couples:2].set(donor - passed).at[2:2 + 2 * couples:2].set(sink + passed)
    return tallies[jax.random.permutation(jax.random.fold_in(rng, 2), number_of)]


def noise(stream_key, dims, scale, limit, cuts=(), kind=jnp.bfloat16):
    entries = jax.random.normal(stream_key, dims, jnp.float32) * scale
    if len(cuts) > 0:
        entries = steps_of(stream_key, dims, cuts, -0.22, 0.18) * entries
    return jnp.clip(entries, min=-limit, max=limit).astype(kind)


def setup_inputs(seed: int = 0, part: int = 0) -> dict:
    keys = jax.random.split(jax.random.key(seed), 21)
    part_splits = jax.random.split(jax.random.fold_in(keys[20], part), 21)
    return {
        "homolog_hidden": draw_homolog_hidden(jax.random.fold_in(jax.random.fold_in(keys[20], part), 71), part),
        "duo_hidden": noise(part_splits[1], (CUT_AMINO_SITES, CUT_AMINO_SITES, DUAL_DIM), 1.0, 6.0, ((0, 4), (1, 4))),
        "homolog_valid_flags": plant((jax.random.randint(part_splits[2], (ALIGN_STRANDS, CUT_AMINO_SITES), 0, 8) < 7).astype(jnp.int32), jax.random.fold_in(part_splits[2], 1), 0, 1),
        "duo_valid_flags": plant((jax.random.randint(part_splits[3], (CUT_AMINO_SITES, CUT_AMINO_SITES), 0, 8) < 7).astype(jnp.int32), jax.random.fold_in(part_splits[3], 1), 0, 1),
        "polymer_labeling": jnp.searchsorted(jnp.cumsum(uneven_parts(part_splits[4], 4, CUT_AMINO_SITES, CUT_AMINO_SITES // 2, 0)), jnp.arange(CUT_AMINO_SITES), side="right").astype(jnp.int32),
        "monomer_serials": draw_monomer_serials(jax.random.fold_in(jax.random.fold_in(keys[20], part), 71), part),
        "separation_bin_vectors": noise(keys[6], (REL_BINS, DUAL_DIM), 0.5, 4.0),
        "duo_logit_rescale": jnp.clip(1.0 + 0.15 * jax.random.normal(keys[7], (DUAL_DIM,), jnp.float32), 0.25, 1.75),
        "duo_logit_projector": noise(keys[8], (DUAL_DIM, FOCUS_GROUPS), DUAL_DIM ** -0.5, 0.5),
        "homolog_heeded_rescale": jnp.clip(1.0 + 0.15 * jax.random.normal(keys[9], (ALIGN_FEATURES,), jnp.float32), 0.25, 1.75),
        "qkv_valve_projectors": draw_qkv_valve_projectors(jax.random.fold_in(keys[20], 71), part),
        "heeded_exit_projector": noise(keys[11], (ALIGN_FEATURES, ALIGN_FEATURES), ALIGN_FEATURES ** -0.5, 0.375),
        "dyadic_rescale": jnp.clip(1.0 + 0.15 * jax.random.normal(keys[12], (ALIGN_FEATURES,), jnp.float32), 0.25, 1.75),
        "dyadic_factor_projector": noise(keys[13], (ALIGN_FEATURES, 2 * TENSORED_FEATS), ALIGN_FEATURES ** -0.5, 0.375),
        "dyadic_exit_projector": noise(keys[14], (TENSORED_FEATS * TENSORED_FEATS, DUAL_DIM), (TENSORED_FEATS * TENSORED_FEATS // 64) ** -0.5, 1.5),
        "triad_entry_rescales": jnp.clip(1.0 + 0.15 * jax.random.normal(keys[15], (2, DUAL_DIM), jnp.float32), 0.25, 1.75),
        "triad_entry_projectors": noise(keys[16], (2, DUAL_DIM, 4 * TRIAD_DIM), DUAL_DIM ** -0.5, 0.5),
        "triad_valve_projectors": noise(keys[17], (2, DUAL_DIM, DUAL_DIM), DUAL_DIM ** -0.5, 0.5),
        "triad_exit_rescales": jnp.clip(1.0 + 0.15 * jax.random.normal(keys[18], (2, TRIAD_DIM), jnp.float32), 0.25, 1.75),
        "triad_exit_projectors": noise(keys[19], (2, TRIAD_DIM, DUAL_DIM), TRIAD_DIM ** -0.5, 0.5),
    }


norm_eps = 1e-05
mask_big = 1000000000.0
count_eps = 0.001

def quantized_entries(values):
    return lax.optimization_barrier(values.astype(jnp.bfloat16))

def standardize_features(values, norm_gain):
    values = values.astype(jnp.float32)
    mean_val = lax.optimization_barrier(jnp.mean(values, axis=-1, keepdims=True))
    centred = values - mean_val
    spread = lax.optimization_barrier(jnp.mean(centred * centred, axis=-1, keepdims=True))
    return centred * lax.rsqrt(spread + norm_eps) * norm_gain.astype(jnp.float32)

def unrolled_tensored_term(values, weight):
    lead_shape = values.shape[:-1]
    flat_out = jnp.dot(values.reshape(-1, values.shape[-1]), weight, preferred_element_type=jnp.float32)
    return flat_out.reshape(lead_shape + (weight.shape[1],))

def threeway_update(duo_hidden_values, duo_valid_flags, norm_gain, w_in, w_gate, out_gain, w_out, incoming):
    tri_normed = quantized_entries(standardize_features(duo_hidden_values, norm_gain))
    mapped_contents = unrolled_tensored_term(tri_normed, w_in)
    width_tri = w_in.shape[1] // 4
    mask_as_float = duo_valid_flags.astype(jnp.float32)[..., None]
    left_fac = quantized_entries(jax.nn.sigmoid(mapped_contents[..., width_tri:2 * width_tri]) * mapped_contents[..., :width_tri] * mask_as_float)
    right_fac = quantized_entries(jax.nn.sigmoid(mapped_contents[..., 3 * width_tri:]) * mapped_contents[..., 2 * width_tri:3 * width_tri] * mask_as_float)
    if incoming:
        einsum_form = 'kic,kjc->ijc'
    else:
        einsum_form = 'ikc,jkc->ijc'
    product = quantized_entries(jnp.einsum(einsum_form, left_fac.astype(jnp.float32), right_fac.astype(jnp.float32), precision=lax.Precision.HIGHEST))
    product_normed = quantized_entries(standardize_features(product, out_gain))
    sigmoid_switches = jax.nn.sigmoid(unrolled_tensored_term(tri_normed, w_gate))
    return duo_hidden_values + sigmoid_switches * unrolled_tensored_term(product_normed, w_out)

def reference(homolog_hidden, duo_hidden, homolog_valid_flags, duo_valid_flags, polymer_labeling, monomer_serials, separation_bin_vectors, duo_logit_rescale, duo_logit_projector, homolog_heeded_rescale, qkv_valve_projectors, heeded_exit_projector, dyadic_rescale, dyadic_factor_projector, dyadic_exit_projector, triad_entry_rescales, triad_entry_projectors, triad_valve_projectors, triad_exit_rescales, triad_exit_projectors):
    rel_reach = (REL_BINS - 2) // 2
    offset = jnp.clip(monomer_serials[:, None] - monomer_serials[None, :], -rel_reach, rel_reach) + rel_reach
    rel_bins = jnp.where(polymer_labeling[:, None] == polymer_labeling[None, :], offset, REL_BINS - 1).astype(jnp.int32)
    duo_hidden_values = duo_hidden.astype(jnp.float32) + separation_bin_vectors.astype(jnp.float32)[rel_bins]
    pair_normed = quantized_entries(standardize_features(duo_hidden_values, duo_logit_rescale))
    pair_bias = jnp.transpose(quantized_entries(unrolled_tensored_term(pair_normed, duo_logit_projector)), (2, 0, 1)).astype(jnp.float32)
    lineup_standardized = quantized_entries(standardize_features(homolog_hidden, homolog_heeded_rescale))
    mapped_contents = unrolled_tensored_term(lineup_standardized, qkv_valve_projectors)
    asking_array = quantized_entries(mapped_contents[..., :ALIGN_FEATURES] * GROUP_CHANNEL ** (-0.5))
    lookup_strand_lines = quantized_entries(mapped_contents[..., ALIGN_FEATURES:2 * ALIGN_FEATURES])
    content_strand_lines = quantized_entries(mapped_contents[..., 2 * ALIGN_FEATURES:3 * ALIGN_FEATURES])
    sigmoid_switches = jax.nn.sigmoid(mapped_contents[..., 3 * ALIGN_FEATURES:])

    def attend_single_row(row_args):
        query_row, key_row, value_row, mask_row = row_args
        query_heads = query_row.astype(jnp.float32).reshape(CUT_AMINO_SITES, FOCUS_GROUPS, GROUP_CHANNEL)
        key_per_head = key_row.astype(jnp.float32).reshape(CUT_AMINO_SITES, FOCUS_GROUPS, GROUP_CHANNEL)
        value_per_head = value_row.astype(jnp.float32).reshape(CUT_AMINO_SITES, FOCUS_GROUPS, GROUP_CHANNEL)
        scores = jnp.einsum('ihd,jhd->hij', query_heads, key_per_head, precision=lax.Precision.HIGHEST)
        scores = scores + pair_bias + ((mask_row.astype(jnp.float32) - 1.0) * mask_big)[None, None, :]
        row_max = lax.optimization_barrier(jnp.max(scores, axis=-1, keepdims=True))
        weights = jnp.exp(scores - row_max)
        row_sum = lax.optimization_barrier(jnp.sum(weights, axis=-1))
        weights_bf = quantized_entries(weights).astype(jnp.float32)
        focused_readout = jnp.einsum('hij,jhd->ihd', weights_bf, value_per_head, precision=lax.Precision.HIGHEST)
        focused_readout = focused_readout / jnp.transpose(row_sum)[:, :, None]
        return focused_readout.reshape(CUT_AMINO_SITES, ALIGN_FEATURES)
    focused_readout = lax.map(attend_single_row, (asking_array, lookup_strand_lines, content_strand_lines, homolog_valid_flags))
    merged_focus_groups = quantized_entries(sigmoid_switches * focused_readout)
    lineup_updated_state = (homolog_hidden.astype(jnp.float32) + unrolled_tensored_term(merged_focus_groups, heeded_exit_projector)).astype(jnp.bfloat16)
    outer_product_normalized = quantized_entries(standardize_features(lineup_updated_state, dyadic_rescale))
    mask_as_float = homolog_valid_flags.astype(jnp.float32)
    factors = unrolled_tensored_term(outer_product_normalized, dyadic_factor_projector) * mask_as_float[..., None]
    left_fac = quantized_entries(factors[..., :TENSORED_FEATS]).astype(jnp.float32)
    right_fac = quantized_entries(factors[..., TENSORED_FEATS:]).astype(jnp.float32)
    counts = jnp.einsum('si,sj->ij', mask_as_float, mask_as_float, precision=lax.Precision.HIGHEST)
    row_block = 16

    def outer_rows(first_row):
        left_factor_rows = lax.dynamic_slice_in_dim(left_fac, first_row, row_block, 1)
        outer_prod = quantized_entries(jnp.einsum('sic,sjd->ijcd', left_factor_rows, right_fac, precision=lax.Precision.HIGHEST)).astype(jnp.float32)
        outer_prod = outer_prod.reshape(row_block, CUT_AMINO_SITES, TENSORED_FEATS * TENSORED_FEATS)
        return jnp.einsum('ijk,kz->ijz', outer_prod, dyadic_exit_projector.astype(jnp.float32), precision=lax.Precision.HIGHEST)
    first_rows = jnp.arange(CUT_AMINO_SITES // row_block, dtype=jnp.int32) * row_block
    update = lax.map(outer_rows, first_rows).reshape(CUT_AMINO_SITES, CUT_AMINO_SITES, DUAL_DIM)
    duo_hidden_values = duo_hidden_values + update / (count_eps + counts)[..., None]
    for threefold_module in range(2):
        duo_hidden_values = threeway_update(duo_hidden_values, duo_valid_flags, triad_entry_rescales[threefold_module], triad_entry_projectors[threefold_module], triad_valve_projectors[threefold_module], triad_exit_rescales[threefold_module], triad_exit_projectors[threefold_module], threefold_module == 1)
    return (lineup_updated_state, duo_hidden_values.astype(jnp.bfloat16))
```

```python
import jax
import jax.numpy as jnp
from jax import lax
from jax.sharding import PartitionSpec as P

REL_BINS = 66


norm_eps = 1e-05
mask_big = 1000000000.0
count_eps = 0.001


def standardize_features(values, norm_gain, norm_axis):
    values = values.astype(jnp.float32)
    mean_val = jnp.mean(values, axis=norm_axis, keepdims=True)
    centred = values - mean_val
    spread = jnp.mean(centred * centred, axis=norm_axis, keepdims=True)
    return centred * lax.rsqrt(spread + norm_eps) * norm_gain


def threeway_update(
    duo_hidden_values, duo_valid_flags, norm_gain, w_in, w_gate, out_gain, w_out, incoming
):
    width_tri = w_in.shape[1] // 4
    rows, cols = duo_valid_flags.shape
    tri_normed = standardize_features(duo_hidden_values, norm_gain, 2).astype(jnp.bfloat16)
    flags = duo_valid_flags.astype(jnp.float32)
    if incoming:
        positions = jnp.transpose(tri_normed, (1, 0, 2))
        flags = flags.T
        share_axis, spread_axis = ("branch", "tile"), "dap"
        kept, summed = cols, rows
    else:
        positions = tri_normed
        share_axis, spread_axis = "dap", ("branch", "tile")
        kept, summed = rows, cols
    positions = positions.reshape(kept * summed, width_tri)
    flags = flags.reshape(1, kept * summed)
    shares = lax.axis_size(share_axis)
    share = width_tri // shares
    mapped = jnp.einsum("pc,cd->dp", positions, w_in, preferred_element_type=jnp.float32)
    blocks = [mapped[n * width_tri : (n + 1) * width_tri] for n in range(4)]
    left_fac = (jax.nn.sigmoid(blocks[1]) * blocks[0] * flags).astype(jnp.bfloat16)
    right_fac = (jax.nn.sigmoid(blocks[3]) * blocks[2] * flags).astype(jnp.bfloat16)

    def by_channel_share(factor):
        got = lax.all_to_all(
            factor.reshape(shares, share, kept * summed), share_axis, split_axis=0, concat_axis=0
        )
        got = got.reshape(shares, share, kept, summed)
        return jnp.transpose(got, (1, 2, 0, 3)).reshape(share, kept, shares * summed)

    if incoming:
        left_own = by_channel_share(left_fac)
        left_all = lax.all_gather(left_own, spread_axis, axis=0)
        right_own = by_channel_share(right_fac)
        product = jnp.einsum(
            "gcik,cjk->gicj", left_all, right_own, preferred_element_type=jnp.float32
        ).astype(jnp.bfloat16)
        product = product.reshape(shares, rows, share, cols)
        product = jnp.transpose(product, (0, 2, 1, 3))
    else:
        right_own = by_channel_share(right_fac)
        right_all = lax.all_gather(right_own, spread_axis, axis=0)
        left_own = by_channel_share(left_fac)
        product = jnp.einsum(
            "cik,gcjk->gjci", left_own, right_all, preferred_element_type=jnp.float32
        ).astype(jnp.bfloat16)
        product = product.reshape(shares, cols, share, rows)
        product = jnp.transpose(product, (0, 2, 3, 1))
    merged = lax.all_to_all(
        product.reshape(shares, share, rows * cols), share_axis, split_axis=0, concat_axis=0
    ).reshape(width_tri, rows * cols)
    sigmoid_switches = jax.nn.sigmoid(
        jnp.einsum("ijc,cd->ijd", tri_normed, w_gate, preferred_element_type=jnp.float32)
    )
    product_normed = standardize_features(merged, out_gain[:, None], 0).astype(jnp.bfloat16)
    update = jnp.einsum("cp,cz->pz", product_normed, w_out, preferred_element_type=jnp.float32)
    return duo_hidden_values + sigmoid_switches * update.reshape(rows, cols, width_tri)


def body(
    homolog_hidden,
    duo_hidden,
    homolog_valid_flags,
    duo_valid_flags,
    polymer_labeling,
    monomer_serials,
    separation_bin_vectors,
    duo_logit_rescale,
    duo_logit_projector,
    homolog_heeded_rescale,
    qkv_valve_projectors,
    heeded_exit_projector,
    dyadic_rescale,
    dyadic_factor_projector,
    dyadic_exit_projector,
    triad_entry_rescales,
    triad_entry_projectors,
    triad_valve_projectors,
    triad_exit_rescales,
    triad_exit_projectors,
):
    lines_each_shard, sites_each_shard, lineup_feature_extent = homolog_hidden.shape
    columns_per_device = duo_hidden.shape[1]
    number_of_heads = duo_logit_projector.shape[1]
    head_channels = lineup_feature_extent // number_of_heads
    outer_channels = dyadic_factor_projector.shape[1] // 2
    row_start = lax.axis_index(("branch", "tile")) * sites_each_shard
    col_start = lax.axis_index("dap") * columns_per_device
    rel_reach = (REL_BINS - 2) // 2
    res_rows = lax.dynamic_slice_in_dim(monomer_serials, row_start, sites_each_shard)
    res_cols = lax.dynamic_slice_in_dim(monomer_serials, col_start, columns_per_device)
    chain_rows = lax.dynamic_slice_in_dim(polymer_labeling, row_start, sites_each_shard)
    chain_cols = lax.dynamic_slice_in_dim(polymer_labeling, col_start, columns_per_device)
    offset = jnp.clip(res_rows[:, None] - res_cols[None, :], -rel_reach, rel_reach) + rel_reach
    rel_bins = jnp.where(chain_rows[:, None] == chain_cols[None, :], offset, REL_BINS - 1)
    one_hot = (rel_bins[:, :, None] == jnp.arange(REL_BINS, dtype=jnp.int32)[None, None, :]).astype(
        jnp.bfloat16
    )
    duo_hidden_values = duo_hidden.astype(jnp.float32) + jnp.einsum(
        "ijb,bc->ijc", one_hot, separation_bin_vectors, preferred_element_type=jnp.float32
    )
    pair_normed = standardize_features(duo_hidden_values, duo_logit_rescale, 2).astype(jnp.bfloat16)
    local_bias = jnp.einsum(
        "ijc,ch->hij", pair_normed, duo_logit_projector, preferred_element_type=jnp.float32
    ).astype(jnp.bfloat16)
    row_bias = lax.all_gather(
        local_bias.reshape(number_of_heads, sites_each_shard * columns_per_device), "dap", axis=0
    ).reshape(-1, number_of_heads, sites_each_shard, columns_per_device)
    row_bias = jnp.transpose(row_bias, (1, 2, 0, 3)).reshape(number_of_heads, sites_each_shard, -1)
    mask_grid = lax.all_gather(
        homolog_valid_flags.astype(jnp.bfloat16), ("dap", "branch", "tile"), axis=0
    ).reshape(lax.axis_size("dap"), -1, lines_each_shard, sites_each_shard)
    mask_grid = jnp.transpose(mask_grid, (0, 2, 1, 3)).reshape(
        lax.axis_size("dap") * lines_each_shard, -1
    )
    lineup_standardized = standardize_features(homolog_hidden, homolog_heeded_rescale, 2).astype(
        jnp.bfloat16
    )
    mapped_contents = jnp.einsum(
        "ezp,pb->ezb", lineup_standardized, qkv_valve_projectors, preferred_element_type=jnp.float32
    )
    asking_array = (mapped_contents[..., :lineup_feature_extent] * head_channels ** (-0.5)).astype(
        jnp.bfloat16
    )
    asking_array = asking_array.reshape(
        lines_each_shard, sites_each_shard, number_of_heads, head_channels
    )
    key_value_pairs = mapped_contents[
        ..., lineup_feature_extent : 3 * lineup_feature_extent
    ].astype(jnp.bfloat16)
    sigmoid_switches = jax.nn.sigmoid(mapped_contents[..., 3 * lineup_feature_extent :])
    run_max = jnp.full((lines_each_shard, number_of_heads, sites_each_shard), -jnp.inf, jnp.float32)
    run_sum = jnp.zeros((lines_each_shard, number_of_heads, sites_each_shard), jnp.float32)
    run_acc = jnp.zeros(
        (lines_each_shard, number_of_heads, sites_each_shard, head_channels), jnp.float32
    )
    key_value_slice = lax.all_gather(key_value_pairs, ("branch", "tile"), axis=1, tiled=True)
    mask_piece = lax.dynamic_slice_in_dim(
        mask_grid, lax.axis_index("dap") * lines_each_shard, lines_each_shard, axis=0
    )
    slice_length = key_value_slice.shape[1]
    key_per_head = key_value_slice[..., :lineup_feature_extent].reshape(
        lines_each_shard, slice_length, number_of_heads, head_channels
    )
    value_per_head = key_value_slice[..., lineup_feature_extent:].reshape(
        lines_each_shard, slice_length, number_of_heads, head_channels
    )
    key_bias = row_bias.astype(jnp.float32)
    scores = jnp.einsum(
        "sihd,sjhd->shij", asking_array, key_per_head, preferred_element_type=jnp.float32
    )
    scores = (
        scores
        + key_bias[None]
        + ((mask_piece.astype(jnp.float32) - 1.0) * mask_big)[:, None, None, :]
    )
    new_max = jnp.max(scores, axis=-1)
    old_scale = jnp.exp(run_max - new_max)
    weights = jnp.exp(scores - new_max[..., None])
    run_sum = run_sum * old_scale + jnp.sum(weights, axis=-1)
    run_acc = run_acc * old_scale[..., None] + jnp.einsum(
        "shij,sjhd->shid",
        weights.astype(jnp.bfloat16),
        value_per_head,
        preferred_element_type=jnp.float32,
    )
    run_max, run_sum, run_acc = (new_max, run_sum, run_acc)
    focused_readout = run_acc / run_sum[..., None]
    focused_readout = jnp.transpose(focused_readout, (0, 2, 1, 3)).reshape(
        lines_each_shard, sites_each_shard, lineup_feature_extent
    )
    merged_focus_groups = (sigmoid_switches * focused_readout).astype(jnp.bfloat16)
    lineup_updated_state = (
        homolog_hidden.astype(jnp.float32)
        + jnp.einsum(
            "ezp,pb->ezb",
            merged_focus_groups,
            heeded_exit_projector,
            preferred_element_type=jnp.float32,
        )
    ).astype(jnp.bfloat16)
    outer_product_normalized = standardize_features(lineup_updated_state, dyadic_rescale, 2).astype(
        jnp.bfloat16
    )
    factors = (
        jnp.einsum(
            "ezp,pb->ezb",
            outer_product_normalized,
            dyadic_factor_projector,
            preferred_element_type=jnp.float32,
        )
        * homolog_valid_flags.astype(jnp.float32)[..., None]
    )
    factors = factors.astype(jnp.bfloat16)
    all_factors = lax.all_gather(factors, ("dap", "branch", "tile"), axis=0).reshape(
        lax.axis_size("dap"), -1, lines_each_shard, sites_each_shard, 2 * outer_channels
    )
    alignment_rows = mask_grid.shape[0]
    left_rows = lax.dynamic_index_in_dim(
        all_factors, lax.axis_index(("branch", "tile")), axis=1, keepdims=False
    )[..., :outer_channels].reshape(alignment_rows, sites_each_shard, outer_channels)
    block = col_start // sites_each_shard
    right_rows = lax.dynamic_index_in_dim(all_factors, block, axis=1, keepdims=False)[
        ..., outer_channels:
    ].reshape(alignment_rows, sites_each_shard, outer_channels)
    right_rows = lax.dynamic_slice_in_dim(
        right_rows, col_start - block * sites_each_shard, columns_per_device, axis=1
    )
    mask_rows = lax.dynamic_slice_in_dim(mask_grid, row_start, sites_each_shard, axis=1)
    mask_right = lax.dynamic_slice_in_dim(mask_grid, col_start, columns_per_device, axis=1)
    counts = jnp.einsum("si,sj->ij", mask_rows, mask_right, preferred_element_type=jnp.float32)
    exit_by_channel = dyadic_exit_projector.reshape(outer_channels, outer_channels, -1)
    spread_right = jnp.einsum(
        "sjd,cdz->scjz", right_rows, exit_by_channel, preferred_element_type=jnp.float32
    ).astype(jnp.bfloat16)
    update = jnp.einsum(
        "sic,scjz->ijz", left_rows, spread_right, preferred_element_type=jnp.float32
    )
    duo_hidden_values = duo_hidden_values + update / (count_eps + counts)[..., None]
    for threefold_module in range(2):
        duo_hidden_values = threeway_update(
            duo_hidden_values,
            duo_valid_flags,
            triad_entry_rescales[threefold_module],
            triad_entry_projectors[threefold_module],
            triad_valve_projectors[threefold_module],
            triad_exit_rescales[threefold_module],
            triad_exit_projectors[threefold_module],
            threefold_module == 1,
        )
    return (lineup_updated_state, duo_hidden_values.astype(jnp.bfloat16))


def solution(mesh):
    placed = (
        P(("groups", "dap"), ("branch", "tile"), None),
        P(("groups", "branch", "tile"), "dap", None),
        P(("groups", "dap"), ("branch", "tile")),
        P(("groups", "branch", "tile"), "dap"),
        P("groups"),
        P("groups"),
        P(),
        P(),
        P(),
        P(),
        P(),
        P(),
        P(),
        P(),
        P(),
        P(),
        P(),
        P(),
        P(),
        P(),
    )
    return jax.shard_map(
        body,
        mesh=mesh,
        in_specs=placed,
        out_specs=(
            P(("groups", "dap"), ("branch", "tile"), None),
            P(("groups", "branch", "tile"), "dap", None),
        ),
        check_vma=False,
    )
```

```python
import functools

import jax
import jax.numpy as jnp
from jax import lax
from jax.experimental import pallas as pl
from jax.experimental.pallas import tpu as pltpu
from jax.sharding import PartitionSpec as P

REL_BINS = 66


norm_eps = 1e-05
mask_big = 1000000000.0
count_eps = 0.001


def standardize_features(values, norm_gain, norm_axis):
    values = values.astype(jnp.float32)
    mean_val = jnp.mean(values, axis=norm_axis, keepdims=True)
    centred = values - mean_val
    spread = jnp.mean(centred * centred, axis=norm_axis, keepdims=True)
    return centred * lax.rsqrt(spread + norm_eps) * norm_gain


def threeway_update(
    duo_hidden_values, duo_valid_flags, norm_gain, w_in, w_gate, out_gain, w_out, incoming
):
    width_tri = w_in.shape[1] // 4
    rows, cols = duo_valid_flags.shape
    tri_normed = standardize_features(duo_hidden_values, norm_gain, 2).astype(jnp.bfloat16)
    flags = duo_valid_flags.astype(jnp.float32)
    if incoming:
        positions = jnp.transpose(tri_normed, (1, 0, 2))
        flags = flags.T
        share_axis, spread_axis = ("branch", "tile"), "dap"
        kept, summed = cols, rows
    else:
        positions = tri_normed
        share_axis, spread_axis = "dap", ("branch", "tile")
        kept, summed = rows, cols
    positions = positions.reshape(kept * summed, width_tri)
    flags = flags.reshape(1, kept * summed)
    shares = lax.axis_size(share_axis)
    share = width_tri // shares
    mapped = jnp.einsum("pc,cd->dp", positions, w_in, preferred_element_type=jnp.float32)
    blocks = [mapped[n * width_tri : (n + 1) * width_tri] for n in range(4)]
    left_fac = (jax.nn.sigmoid(blocks[1]) * blocks[0] * flags).astype(jnp.bfloat16)
    right_fac = (jax.nn.sigmoid(blocks[3]) * blocks[2] * flags).astype(jnp.bfloat16)

    def by_channel_share(factor):
        got = lax.all_to_all(
            factor.reshape(shares, share, kept * summed), share_axis, split_axis=0, concat_axis=0
        )
        got = got.reshape(shares, share, kept, summed)
        return jnp.transpose(got, (1, 2, 0, 3)).reshape(share, kept, shares * summed)

    if incoming:
        left_own = by_channel_share(left_fac)
        left_all = lax.all_gather(left_own, spread_axis, axis=0)
        right_own = by_channel_share(right_fac)
        product = jnp.einsum(
            "gcik,cjk->gicj", left_all, right_own, preferred_element_type=jnp.float32
        ).astype(jnp.bfloat16)
        product = product.reshape(shares, rows, share, cols)
        product = jnp.transpose(product, (0, 2, 1, 3))
    else:
        right_own = by_channel_share(right_fac)
        right_all = lax.all_gather(right_own, spread_axis, axis=0)
        left_own = by_channel_share(left_fac)
        product = jnp.einsum(
            "cik,gcjk->gjci", left_own, right_all, preferred_element_type=jnp.float32
        ).astype(jnp.bfloat16)
        product = product.reshape(shares, cols, share, rows)
        product = jnp.transpose(product, (0, 2, 3, 1))
    merged = lax.all_to_all(
        product.reshape(shares, share, rows * cols), share_axis, split_axis=0, concat_axis=0
    ).reshape(width_tri, rows * cols)
    sigmoid_switches = jax.nn.sigmoid(
        jnp.einsum("ijc,cd->ijd", tri_normed, w_gate, preferred_element_type=jnp.float32)
    )
    product_normed = standardize_features(merged, out_gain[:, None], 0).astype(jnp.bfloat16)
    update = jnp.einsum("cp,cz->pz", product_normed, w_out, preferred_element_type=jnp.float32)
    return duo_hidden_values + sigmoid_switches * update.reshape(rows, cols, width_tri)


MESH = pl.DeviceIdType.MESH
LANES = 128


def start_remote(src, dst, send_sem, recv_sem, device):
    copy = pltpu.make_async_remote_copy(
        src_ref=src,
        dst_ref=dst,
        send_sem=send_sem,
        recv_sem=recv_sem,
        device_id=device,
        device_id_type=MESH,
    )
    copy.start()
    return copy


def triangle_kernel(
    incoming,
    own_in,
    spread_in,
    state,
    normed,
    w_gate,
    out_gain,
    w_out,
    out,
    own,
    spread,
    own_wide,
    spread_wide,
    product_wide,
    outgoing_blocks,
    merged,
    trade_send,
    trade_recv,
    local_sem,
    spread_send,
    spread_recv,
    back_send,
    back_recv,
):
    n, pairs, share = own.shape[0], own.shape[1], own.shape[2]
    m = spread.shape[0]
    half = LANES // 2
    tiles = lax.axis_size("tile")
    branch, tile, dap = lax.axis_index("branch"), lax.axis_index("tile"), lax.axis_index("dap")
    block = branch * tiles + tile

    def by_block(index):
        return {"branch": index // tiles, "tile": lax.rem(index, tiles)}

    def by_dap(index):
        return {"dap": index}

    if incoming:
        me, trade_to, place, spread_to = block, by_block, dap, by_dap
    else:
        me, trade_to, place, spread_to = dap, by_dap, block, by_block

    barrier = pltpu.get_barrier_semaphore()
    for k in range(1, n):
        pl.semaphore_signal(
            barrier, inc=1, device_id=trade_to(lax.rem(me + k, n)), device_id_type=MESH
        )
    for k in range(1, m):
        pl.semaphore_signal(
            barrier, inc=1, device_id=spread_to(lax.rem(place + k, m)), device_id_type=MESH
        )
    pl.semaphore_wait(barrier, n + m - 2)

    def channels(ref, index):
        return ref.at[:, pl.ds(pl.multiple_of(index * share, share), share), :]

    trades = [[], []]
    for which, (src, dst) in enumerate(((spread_in, spread.at[place, me]), (own_in, own.at[me]))):
        for k in range(1, n):
            to = lax.rem(me + k, n)
            trades[which].append(
                start_remote(
                    channels(src, to),
                    dst,
                    trade_send.at[which, k - 1],
                    trade_recv.at[which, k - 1],
                    trade_to(to),
                )
            )
    locals_ = [
        pltpu.make_async_copy(channels(spread_in, me), spread.at[place, me], local_sem.at[0]),
        pltpu.make_async_copy(channels(own_in, me), own.at[me], local_sem.at[1]),
    ]
    for copy in locals_:
        copy.start()

    def widen(dst, load):
        def step(s, _):
            dst[pl.ds(pl.multiple_of(s * pairs * share, share), pairs * share), :] = (
                load(s).astype(jnp.float32).reshape(pairs * share, LANES)
            )
            return 0

        lax.fori_loop(0, n, step, 0)

    def matrix(ref, c):
        lower = lax.broadcasted_iota(jnp.int32, (pairs, LANES), 1) < half
        columns = []
        for s in range(0, n, 2):
            first = ref[pl.ds(s * pairs * share + c, pairs, stride=share), :]
            second = ref[pl.ds((s + 1) * pairs * share + c, pairs, stride=share), :]
            top = jnp.where(lower, first, pltpu.roll(second, half, 1))
            bottom = jnp.where(lower, pltpu.roll(first, half, 1), second)
            columns.append(jnp.concatenate([top, bottom], axis=0))
        return jnp.concatenate(columns, axis=1).astype(jnp.bfloat16)

    def multiply(g):
        widen(spread_wide, lambda s: spread[g, s])

        def step(c, _):
            mine, other = matrix(own_wide, c), matrix(spread_wide, c)
            left, right = (other, mine) if incoming else (mine, other)
            found = lax.dot_general(
                left, right, (((1,), (1,)), ((), ())), preferred_element_type=jnp.float32
            )
            product_wide[pl.ds(c, pairs, stride=share), :] = jnp.concatenate(
                [found[:pairs], found[pairs:]], axis=1
            )
            return 0

        lax.fori_loop(0, share, step, 0, unroll=4)
        outgoing_blocks[g] = (
            product_wide[...].reshape(pairs, share, LANES).astype(jnp.bfloat16)
        )

        @pl.when(g != me)
        def _():
            start_remote(
                outgoing_blocks.at[g],
                merged.at[me],
                back_send.at[g],
                back_recv.at[me],
                trade_to(g),
            )

        @pl.when(g == me)
        def _():
            merged[g] = outgoing_blocks[g]

    def spread_copy(g, k, slot, device):
        piece = spread.at[g, lax.rem(me - k + n, n)]
        return pltpu.make_async_remote_copy(
            src_ref=piece,
            dst_ref=piece,
            send_sem=spread_send.at[slot, k],
            recv_sem=spread_recv.at[slot, k],
            device_id=device,
            device_id_type=MESH,
        )

    def finish_own():
        locals_[1].wait()
        for copy in trades[1]:
            copy.wait()
        widen(own_wide, lambda s: own[s])

    if incoming:
        right, left = place + 1, place - 1
        has_right, has_left = right < m, left >= 0
        sides = ((0, 1, right, has_right), (1, -1, left, has_left))
        for k in range(n):
            if k == 0:
                locals_[0].wait()
            else:
                trades[0][k - 1].wait()
            for side, _, to, there in sides:

                @pl.when(there)
                def _(side=side, to=to, k=k):
                    spread_copy(place, k, side * (m - 1), spread_to(to)).start()

        finish_own()
        multiply(place)
        for h in range(1, m):
            for side, sign, to, there in sides:
                g = place - sign * h
                has_block = (g >= 0) if sign > 0 else (g < m)

                @pl.when(has_block)
                def _(side=side, to=to, there=there, g=g, h=h):
                    for k in range(n):
                        spread_copy(
                            g, k, side * (m - 1) + h - 1, spread_to(lax.rem(place + 1, m))
                        ).wait_recv()
                        if h < m - 1:

                            @pl.when(there)
                            def _(k=k):
                                spread_copy(g, k, side * (m - 1) + h, spread_to(to)).start()

            for side, sign, to, there in sides:
                g = place - sign * h
                has_block = (g >= 0) if sign > 0 else (g < m)

                @pl.when(has_block)
                def _(g=g):
                    multiply(g)

        for side, sign, to, there in sides:
            for h in range(m - 1):
                g = place - sign * h
                has_block = (g >= 0) if sign > 0 else (g < m)

                @pl.when(jnp.logical_and(there, has_block))
                def _(side=side, g=g, h=h, to=to):
                    for k in range(n):
                        spread_copy(g, k, side * (m - 1) + h, spread_to(to)).wait_send()

    else:
        across = (1 - branch) * tiles + tile
        beside = branch * tiles + (1 - tile)
        beyond = (1 - branch) * tiles + (1 - tile)
        to_tile, to_branch = spread_to(beside), spread_to(across)
        copies = []
        for k in range(n):
            if k == 0:
                locals_[0].wait()
            else:
                trades[0][k - 1].wait()
            for slot, device in ((0, to_tile), (1, to_branch)):
                copy = spread_copy(place, k, slot, device)
                copy.start()
                copies.append(copy)
        finish_own()
        for k in range(n):
            spread_copy(beside, k, 0, to_tile).wait_recv()
            copy = spread_copy(beside, k, 2, to_branch)
            copy.start()
            copies.append(copy)
        multiply(place)
        multiply(beside)
        for k in range(n):
            spread_copy(across, k, 1, to_branch).wait_recv()
        multiply(across)
        for k in range(n):
            spread_copy(beyond, k, 2, to_branch).wait_recv()
        multiply(beyond)
        for copy in copies:
            copy.wait_send()

    for k in range(1, n):
        source = lax.rem(me - k + n, n)
        pltpu.make_async_remote_copy(
            src_ref=outgoing_blocks.at[source],
            dst_ref=merged.at[source],
            send_sem=back_send.at[source],
            recv_sem=back_recv.at[source],
            device_id=trade_to(source),
            device_id_type=MESH,
        ).wait()

    def finish(t, _):
        found = merged[:, pl.ds(t, 1)].astype(jnp.float32).reshape(n * share, LANES)
        centred = found - jnp.mean(found, axis=0, keepdims=True)
        spread_of = jnp.mean(centred * centred, axis=0, keepdims=True)
        scaled = (centred * lax.rsqrt(spread_of + norm_eps) * out_gain[...]).astype(jnp.bfloat16)
        update = lax.dot_general(
            scaled, w_out[...], (((0,), (0,)), ((), ())), preferred_element_type=jnp.float32
        )
        for part in range(2):
            i = part * pairs + t
            gate = jax.nn.sigmoid(
                jnp.dot(normed[i], w_gate[...], preferred_element_type=jnp.float32)
            )
            out[i] = (state[i] + gate * update[part * half : (part + 1) * half]).astype(out.dtype)
        return 0

    lax.fori_loop(0, pairs, finish, 0, unroll=2)


def fused_update(
    state, flags, norm_gain, w_in, w_gate, out_gain, w_out, incoming, out_type
):
    width = w_in.shape[1] // 4
    rows, cols = flags.shape
    n = lax.axis_size("dap")
    share, pairs, half = width // n, rows // 2, rows
    normed = standardize_features(state, norm_gain, 2).astype(jnp.bfloat16)
    flags = flags.astype(jnp.float32)
    positions = jnp.transpose(normed, (1, 0, 2)) if incoming else normed
    flags = flags.T if incoming else flags
    positions = positions.reshape(2, pairs, half, width).transpose(1, 0, 2, 3)
    flags = flags.reshape(2, pairs, half).transpose(1, 0, 2).reshape(pairs, 1, LANES)
    mapped = jnp.einsum(
        "tpc,cd->tdp",
        positions.reshape(pairs, LANES, width),
        w_in,
        preferred_element_type=jnp.float32,
    )
    blocks = [mapped[:, q * width : (q + 1) * width] for q in range(4)]
    left = (jax.nn.sigmoid(blocks[1]) * blocks[0] * flags).astype(jnp.bfloat16)
    right = (jax.nn.sigmoid(blocks[3]) * blocks[2] * flags).astype(jnp.bfloat16)
    own, spread = (right, left) if incoming else (left, right)
    slots = 2 * (n - 1)
    vmem = pl.BlockSpec(memory_space=pltpu.VMEM)
    factor = (n, pairs, share, LANES)
    return pl.pallas_call(
        functools.partial(triangle_kernel, incoming),
        out_shape=jax.ShapeDtypeStruct(state.shape, out_type),
        in_specs=[vmem] * 7,
        out_specs=vmem,
        scratch_shapes=[
            pltpu.VMEM(factor, jnp.bfloat16),
            pltpu.VMEM((n, *factor), jnp.bfloat16),
            pltpu.VMEM((n * pairs * share, LANES), jnp.float32),
            pltpu.VMEM((n * pairs * share, LANES), jnp.float32),
            pltpu.VMEM((pairs * share, LANES), jnp.float32),
            pltpu.VMEM(factor, jnp.bfloat16),
            pltpu.VMEM(factor, jnp.bfloat16),
            pltpu.SemaphoreType.DMA((2, n - 1)),
            pltpu.SemaphoreType.DMA((2, n - 1)),
            pltpu.SemaphoreType.DMA((2,)),
            pltpu.SemaphoreType.DMA((slots, n)),
            pltpu.SemaphoreType.DMA((slots, n)),
            pltpu.SemaphoreType.DMA((n,)),
            pltpu.SemaphoreType.DMA((n,)),
        ],
        compiler_params=pltpu.CompilerParams(
            collective_id=1 if incoming else 0,
            has_side_effects=True,
            vmem_limit_bytes=40 * 1024 * 1024,
        ),
        cost_estimate=pl.CostEstimate(
            flops=2 * 256 * rows * cols * width, bytes_accessed=8 << 20, transcendentals=0
        ),
        name="triangle_in" if incoming else "triangle_out",
    )(own, spread, state, normed, w_gate, out_gain.reshape(width, 1), w_out)


def body(
    homolog_hidden,
    duo_hidden,
    homolog_valid_flags,
    duo_valid_flags,
    polymer_labeling,
    monomer_serials,
    separation_bin_vectors,
    duo_logit_rescale,
    duo_logit_projector,
    homolog_heeded_rescale,
    qkv_valve_projectors,
    heeded_exit_projector,
    dyadic_rescale,
    dyadic_factor_projector,
    dyadic_exit_projector,
    triad_entry_rescales,
    triad_entry_projectors,
    triad_valve_projectors,
    triad_exit_rescales,
    triad_exit_projectors,
):
    lines_each_shard, sites_each_shard, lineup_feature_extent = homolog_hidden.shape
    columns_per_device = duo_hidden.shape[1]
    number_of_heads = duo_logit_projector.shape[1]
    head_channels = lineup_feature_extent // number_of_heads
    outer_channels = dyadic_factor_projector.shape[1] // 2
    row_start = lax.axis_index(("branch", "tile")) * sites_each_shard
    col_start = lax.axis_index("dap") * columns_per_device
    rel_reach = (REL_BINS - 2) // 2
    res_rows = lax.dynamic_slice_in_dim(monomer_serials, row_start, sites_each_shard)
    res_cols = lax.dynamic_slice_in_dim(monomer_serials, col_start, columns_per_device)
    chain_rows = lax.dynamic_slice_in_dim(polymer_labeling, row_start, sites_each_shard)
    chain_cols = lax.dynamic_slice_in_dim(polymer_labeling, col_start, columns_per_device)
    offset = jnp.clip(res_rows[:, None] - res_cols[None, :], -rel_reach, rel_reach) + rel_reach
    rel_bins = jnp.where(chain_rows[:, None] == chain_cols[None, :], offset, REL_BINS - 1)
    one_hot = (rel_bins[:, :, None] == jnp.arange(REL_BINS, dtype=jnp.int32)[None, None, :]).astype(
        jnp.bfloat16
    )
    duo_hidden_values = duo_hidden.astype(jnp.float32) + jnp.einsum(
        "ijb,bc->ijc", one_hot, separation_bin_vectors, preferred_element_type=jnp.float32
    )
    pair_normed = standardize_features(duo_hidden_values, duo_logit_rescale, 2).astype(jnp.bfloat16)
    local_bias = jnp.einsum(
        "ijc,ch->hij", pair_normed, duo_logit_projector, preferred_element_type=jnp.float32
    ).astype(jnp.bfloat16)
    row_bias = lax.all_gather(
        local_bias.reshape(number_of_heads, sites_each_shard * columns_per_device), "dap", axis=0
    ).reshape(-1, number_of_heads, sites_each_shard, columns_per_device)
    row_bias = jnp.transpose(row_bias, (1, 2, 0, 3)).reshape(number_of_heads, sites_each_shard, -1)
    mask_grid = lax.all_gather(
        homolog_valid_flags.astype(jnp.bfloat16), ("dap", "branch", "tile"), axis=0
    ).reshape(lax.axis_size("dap"), -1, lines_each_shard, sites_each_shard)
    mask_grid = jnp.transpose(mask_grid, (0, 2, 1, 3)).reshape(
        lax.axis_size("dap") * lines_each_shard, -1
    )
    lineup_standardized = standardize_features(homolog_hidden, homolog_heeded_rescale, 2).astype(
        jnp.bfloat16
    )
    mapped_contents = jnp.einsum(
        "ezp,pb->ezb", lineup_standardized, qkv_valve_projectors, preferred_element_type=jnp.float32
    )
    asking_array = (mapped_contents[..., :lineup_feature_extent] * head_channels ** (-0.5)).astype(
        jnp.bfloat16
    )
    asking_array = asking_array.reshape(
        lines_each_shard, sites_each_shard, number_of_heads, head_channels
    )
    key_value_pairs = mapped_contents[
        ..., lineup_feature_extent : 3 * lineup_feature_extent
    ].astype(jnp.bfloat16)
    sigmoid_switches = jax.nn.sigmoid(mapped_contents[..., 3 * lineup_feature_extent :])
    run_max = jnp.full((lines_each_shard, number_of_heads, sites_each_shard), -jnp.inf, jnp.float32)
    run_sum = jnp.zeros((lines_each_shard, number_of_heads, sites_each_shard), jnp.float32)
    run_acc = jnp.zeros(
        (lines_each_shard, number_of_heads, sites_each_shard, head_channels), jnp.float32
    )
    key_value_slice = lax.all_gather(key_value_pairs, ("branch", "tile"), axis=1, tiled=True)
    mask_piece = lax.dynamic_slice_in_dim(
        mask_grid, lax.axis_index("dap") * lines_each_shard, lines_each_shard, axis=0
    )
    slice_length = key_value_slice.shape[1]
    key_per_head = key_value_slice[..., :lineup_feature_extent].reshape(
        lines_each_shard, slice_length, number_of_heads, head_channels
    )
    value_per_head = key_value_slice[..., lineup_feature_extent:].reshape(
        lines_each_shard, slice_length, number_of_heads, head_channels
    )
    key_bias = row_bias.astype(jnp.float32)
    scores = jnp.einsum(
        "sihd,sjhd->shij", asking_array, key_per_head, preferred_element_type=jnp.float32
    )
    scores = (
        scores
        + key_bias[None]
        + ((mask_piece.astype(jnp.float32) - 1.0) * mask_big)[:, None, None, :]
    )
    new_max = jnp.max(scores, axis=-1)
    old_scale = jnp.exp(run_max - new_max)
    weights = jnp.exp(scores - new_max[..., None])
    run_sum = run_sum * old_scale + jnp.sum(weights, axis=-1)
    run_acc = run_acc * old_scale[..., None] + jnp.einsum(
        "shij,sjhd->shid",
        weights.astype(jnp.bfloat16),
        value_per_head,
        preferred_element_type=jnp.float32,
    )
    run_max, run_sum, run_acc = (new_max, run_sum, run_acc)
    focused_readout = run_acc / run_sum[..., None]
    focused_readout = jnp.transpose(focused_readout, (0, 2, 1, 3)).reshape(
        lines_each_shard, sites_each_shard, lineup_feature_extent
    )
    merged_focus_groups = (sigmoid_switches * focused_readout).astype(jnp.bfloat16)
    lineup_updated_state = (
        homolog_hidden.astype(jnp.float32)
        + jnp.einsum(
            "ezp,pb->ezb",
            merged_focus_groups,
            heeded_exit_projector,
            preferred_element_type=jnp.float32,
        )
    ).astype(jnp.bfloat16)
    outer_product_normalized = standardize_features(lineup_updated_state, dyadic_rescale, 2).astype(
        jnp.bfloat16
    )
    factors = (
        jnp.einsum(
            "ezp,pb->ezb",
            outer_product_normalized,
            dyadic_factor_projector,
            preferred_element_type=jnp.float32,
        )
        * homolog_valid_flags.astype(jnp.float32)[..., None]
    )
    factors = factors.astype(jnp.bfloat16)
    all_factors = lax.all_gather(factors, ("dap", "branch", "tile"), axis=0).reshape(
        lax.axis_size("dap"), -1, lines_each_shard, sites_each_shard, 2 * outer_channels
    )
    alignment_rows = mask_grid.shape[0]
    left_rows = lax.dynamic_index_in_dim(
        all_factors, lax.axis_index(("branch", "tile")), axis=1, keepdims=False
    )[..., :outer_channels].reshape(alignment_rows, sites_each_shard, outer_channels)
    block = col_start // sites_each_shard
    right_rows = lax.dynamic_index_in_dim(all_factors, block, axis=1, keepdims=False)[
        ..., outer_channels:
    ].reshape(alignment_rows, sites_each_shard, outer_channels)
    right_rows = lax.dynamic_slice_in_dim(
        right_rows, col_start - block * sites_each_shard, columns_per_device, axis=1
    )
    mask_rows = lax.dynamic_slice_in_dim(mask_grid, row_start, sites_each_shard, axis=1)
    mask_right = lax.dynamic_slice_in_dim(mask_grid, col_start, columns_per_device, axis=1)
    counts = jnp.einsum("si,sj->ij", mask_rows, mask_right, preferred_element_type=jnp.float32)
    exit_by_channel = dyadic_exit_projector.reshape(outer_channels, outer_channels, -1)
    spread_right = jnp.einsum(
        "sjd,cdz->scjz", right_rows, exit_by_channel, preferred_element_type=jnp.float32
    ).astype(jnp.bfloat16)
    update = jnp.einsum(
        "sic,scjz->ijz", left_rows, spread_right, preferred_element_type=jnp.float32
    )
    duo_hidden_values = duo_hidden_values + update / (count_eps + counts)[..., None]
    square = (
        duo_hidden.shape[:2] == (LANES // 2, LANES // 2)
        and lax.axis_size("branch") == lax.axis_size("tile") == 2
        and lax.axis_size("dap") == 4
    )
    for threefold_module in range(2):
        parameters = (
            triad_entry_rescales[threefold_module],
            triad_entry_projectors[threefold_module],
            triad_valve_projectors[threefold_module],
            triad_exit_rescales[threefold_module],
            triad_exit_projectors[threefold_module],
            threefold_module == 1,
        )
        if square:
            out_type = jnp.bfloat16 if threefold_module == 1 else jnp.float32
            duo_hidden_values = fused_update(
                duo_hidden_values, duo_valid_flags, *parameters, out_type
            )
        else:
            duo_hidden_values = threeway_update(duo_hidden_values, duo_valid_flags, *parameters)
    return (lineup_updated_state, duo_hidden_values.astype(jnp.bfloat16))


def solution(mesh):
    placed = (
        P(("groups", "dap"), ("branch", "tile"), None),
        P(("groups", "branch", "tile"), "dap", None),
        P(("groups", "dap"), ("branch", "tile")),
        P(("groups", "branch", "tile"), "dap"),
        P("groups"),
        P("groups"),
        P(),
        P(),
        P(),
        P(),
        P(),
        P(),
        P(),
        P(),
        P(),
        P(),
        P(),
        P(),
        P(),
        P(),
    )
    return jax.shard_map(
        body,
        mesh=mesh,
        in_specs=placed,
        out_specs=(
            P(("groups", "dap"), ("branch", "tile"), None),
            P(("groups", "branch", "tile"), "dap", None),
        ),
        check_vma=False,
    )
```

```python
import functools

import jax
import jax.numpy as jnp
from jax import lax
from jax.experimental import pallas as pl
from jax.experimental.pallas import tpu as pltpu
from jax.sharding import PartitionSpec as P

REL_BINS = 66


norm_eps = 1e-05
mask_big = 1000000000.0
count_eps = 0.001


def standardize_features(values, norm_gain, norm_axis):
    values = values.astype(jnp.float32)
    mean_val = jnp.mean(values, axis=norm_axis, keepdims=True)
    centred = values - mean_val
    spread = jnp.mean(centred * centred, axis=norm_axis, keepdims=True)
    return centred * lax.rsqrt(spread + norm_eps) * norm_gain


def threeway_update(
    duo_hidden_values, duo_valid_flags, norm_gain, w_in, w_gate, out_gain, w_out, incoming
):
    width_tri = w_in.shape[1] // 4
    rows, cols = duo_valid_flags.shape
    tri_normed = standardize_features(duo_hidden_values, norm_gain, 2).astype(jnp.bfloat16)
    flags = duo_valid_flags.astype(jnp.float32)
    if incoming:
        positions = jnp.transpose(tri_normed, (1, 0, 2))
        flags = flags.T
        share_axis, spread_axis = ("branch", "tile"), "dap"
        kept, summed = cols, rows
    else:
        positions = tri_normed
        share_axis, spread_axis = "dap", ("branch", "tile")
        kept, summed = rows, cols
    positions = positions.reshape(kept * summed, width_tri)
    flags = flags.reshape(1, kept * summed)
    shares = lax.axis_size(share_axis)
    share = width_tri // shares
    mapped = jnp.einsum("pc,cd->dp", positions, w_in, preferred_element_type=jnp.float32)
    blocks = [mapped[n * width_tri : (n + 1) * width_tri] for n in range(4)]
    left_fac = (jax.nn.sigmoid(blocks[1]) * blocks[0] * flags).astype(jnp.bfloat16)
    right_fac = (jax.nn.sigmoid(blocks[3]) * blocks[2] * flags).astype(jnp.bfloat16)

    def by_channel_share(factor):
        got = lax.all_to_all(
            factor.reshape(shares, share, kept * summed), share_axis, split_axis=0, concat_axis=0
        )
        got = got.reshape(shares, share, kept, summed)
        return jnp.transpose(got, (1, 2, 0, 3)).reshape(share, kept, shares * summed)

    if incoming:
        left_own = by_channel_share(left_fac)
        left_all = lax.all_gather(left_own, spread_axis, axis=0)
        right_own = by_channel_share(right_fac)
        product = jnp.einsum(
            "gcik,cjk->gicj", left_all, right_own, preferred_element_type=jnp.float32
        ).astype(jnp.bfloat16)
        product = product.reshape(shares, rows, share, cols)
        product = jnp.transpose(product, (0, 2, 1, 3))
    else:
        right_own = by_channel_share(right_fac)
        right_all = lax.all_gather(right_own, spread_axis, axis=0)
        left_own = by_channel_share(left_fac)
        product = jnp.einsum(
            "cik,gcjk->gjci", left_own, right_all, preferred_element_type=jnp.float32
        ).astype(jnp.bfloat16)
        product = product.reshape(shares, cols, share, rows)
        product = jnp.transpose(product, (0, 2, 3, 1))
    merged = lax.all_to_all(
        product.reshape(shares, share, rows * cols), share_axis, split_axis=0, concat_axis=0
    ).reshape(width_tri, rows * cols)
    sigmoid_switches = jax.nn.sigmoid(
        jnp.einsum("ijc,cd->ijd", tri_normed, w_gate, preferred_element_type=jnp.float32)
    )
    product_normed = standardize_features(merged, out_gain[:, None], 0).astype(jnp.bfloat16)
    update = jnp.einsum("cp,cz->pz", product_normed, w_out, preferred_element_type=jnp.float32)
    return duo_hidden_values + sigmoid_switches * update.reshape(rows, cols, width_tri)


MESH = pl.DeviceIdType.MESH
LANES = 128


def start_remote(src, dst, send_sem, recv_sem, device):
    copy = pltpu.make_async_remote_copy(
        src_ref=src,
        dst_ref=dst,
        send_sem=send_sem,
        recv_sem=recv_sem,
        device_id=device,
        device_id_type=MESH,
    )
    copy.start()
    return copy


def triangle_kernel(
    incoming,
    own_in,
    spread_in,
    state,
    normed,
    w_gate,
    out_gain,
    w_out,
    out,
    own,
    spread,
    own_wide,
    spread_wide,
    product_wide,
    outgoing_blocks,
    merged,
    trade_send,
    trade_recv,
    local_sem,
    spread_send,
    spread_recv,
    back_send,
    back_recv,
):
    n, pairs, share = own.shape[0], own.shape[1], own.shape[2]
    m = spread.shape[0]
    half = LANES // 2
    tiles = lax.axis_size("tile")
    branch, tile, dap = lax.axis_index("branch"), lax.axis_index("tile"), lax.axis_index("dap")
    block = branch * tiles + tile

    def by_block(index):
        return {"branch": index // tiles, "tile": lax.rem(index, tiles)}

    def by_dap(index):
        return {"dap": index}

    if incoming:
        me, trade_to, place, spread_to = block, by_block, dap, by_dap
    else:
        me, trade_to, place, spread_to = dap, by_dap, block, by_block

    barrier = pltpu.get_barrier_semaphore()
    for k in range(1, n):
        pl.semaphore_signal(
            barrier, inc=1, device_id=trade_to(lax.rem(me + k, n)), device_id_type=MESH
        )
    for k in range(1, m):
        pl.semaphore_signal(
            barrier, inc=1, device_id=spread_to(lax.rem(place + k, m)), device_id_type=MESH
        )
    pl.semaphore_wait(barrier, n + m - 2)

    def channels(ref, index):
        return ref.at[:, pl.ds(pl.multiple_of(index * share, share), share), :]

    trades = [[], []]
    for which, (src, dst) in enumerate(((spread_in, spread.at[place, me]), (own_in, own.at[me]))):
        for k in range(1, n):
            to = lax.rem(me + k, n)
            trades[which].append(
                start_remote(
                    channels(src, to),
                    dst,
                    trade_send.at[which, k - 1],
                    trade_recv.at[which, k - 1],
                    trade_to(to),
                )
            )
    locals_ = [
        pltpu.make_async_copy(channels(spread_in, me), spread.at[place, me], local_sem.at[0]),
        pltpu.make_async_copy(channels(own_in, me), own.at[me], local_sem.at[1]),
    ]
    for copy in locals_:
        copy.start()

    def widen(dst, load):
        def step(s, _):
            dst[pl.ds(pl.multiple_of(s * pairs * share, share), pairs * share), :] = (
                load(s).astype(jnp.float32).reshape(pairs * share, LANES)
            )
            return 0

        lax.fori_loop(0, n, step, 0)

    def matrix(ref, c):
        lower = lax.broadcasted_iota(jnp.int32, (pairs, LANES), 1) < half
        columns = []
        for s in range(0, n, 2):
            first = ref[pl.ds(s * pairs * share + c, pairs, stride=share), :]
            second = ref[pl.ds((s + 1) * pairs * share + c, pairs, stride=share), :]
            top = jnp.where(lower, first, pltpu.roll(second, half, 1))
            bottom = jnp.where(lower, pltpu.roll(first, half, 1), second)
            columns.append(jnp.concatenate([top, bottom], axis=0))
        return jnp.concatenate(columns, axis=1).astype(jnp.bfloat16)

    def multiply(g):
        widen(spread_wide, lambda s: spread[g, s])

        def step(c, _):
            mine, other = matrix(own_wide, c), matrix(spread_wide, c)
            left, right = (other, mine) if incoming else (mine, other)
            found = lax.dot_general(
                left, right, (((1,), (1,)), ((), ())), preferred_element_type=jnp.float32
            )
            product_wide[pl.ds(c, pairs, stride=share), :] = jnp.concatenate(
                [found[:pairs], found[pairs:]], axis=1
            )
            return 0

        lax.fori_loop(0, share, step, 0, unroll=4)
        outgoing_blocks[g] = (
            product_wide[...].reshape(pairs, share, LANES).astype(jnp.bfloat16)
        )

        @pl.when(g != me)
        def _():
            start_remote(
                outgoing_blocks.at[g],
                merged.at[me],
                back_send.at[g],
                back_recv.at[me],
                trade_to(g),
            )

        @pl.when(g == me)
        def _():
            merged[g] = outgoing_blocks[g]

    def spread_copy(g, k, slot, device):
        piece = spread.at[g, lax.rem(me - k + n, n)]
        return pltpu.make_async_remote_copy(
            src_ref=piece,
            dst_ref=piece,
            send_sem=spread_send.at[slot, k],
            recv_sem=spread_recv.at[slot, k],
            device_id=device,
            device_id_type=MESH,
        )

    def finish_own():
        locals_[1].wait()
        for copy in trades[1]:
            copy.wait()
        widen(own_wide, lambda s: own[s])

    if incoming:
        right, left = place + 1, place - 1
        has_right, has_left = right < m, left >= 0
        sides = ((0, 1, right, has_right), (1, -1, left, has_left))
        for k in range(n):
            if k == 0:
                locals_[0].wait()
            else:
                trades[0][k - 1].wait()
            for side, _, to, there in sides:

                @pl.when(there)
                def _(side=side, to=to, k=k):
                    spread_copy(place, k, side * (m - 1), spread_to(to)).start()

        finish_own()
        multiply(place)
        for h in range(1, m):
            for side, sign, to, there in sides:
                g = place - sign * h
                has_block = (g >= 0) if sign > 0 else (g < m)

                @pl.when(has_block)
                def _(side=side, to=to, there=there, g=g, h=h):
                    for k in range(n):
                        spread_copy(
                            g, k, side * (m - 1) + h - 1, spread_to(lax.rem(place + 1, m))
                        ).wait_recv()
                        if h < m - 1:

                            @pl.when(there)
                            def _(k=k):
                                spread_copy(g, k, side * (m - 1) + h, spread_to(to)).start()

            for side, sign, to, there in sides:
                g = place - sign * h
                has_block = (g >= 0) if sign > 0 else (g < m)

                @pl.when(has_block)
                def _(g=g):
                    multiply(g)

        for side, sign, to, there in sides:
            for h in range(m - 1):
                g = place - sign * h
                has_block = (g >= 0) if sign > 0 else (g < m)

                @pl.when(jnp.logical_and(there, has_block))
                def _(side=side, g=g, h=h, to=to):
                    for k in range(n):
                        spread_copy(g, k, side * (m - 1) + h, spread_to(to)).wait_send()

    else:
        across = (1 - branch) * tiles + tile
        beside = branch * tiles + (1 - tile)
        beyond = (1 - branch) * tiles + (1 - tile)
        to_tile, to_branch = spread_to(beside), spread_to(across)
        copies = []
        for k in range(n):
            if k == 0:
                locals_[0].wait()
            else:
                trades[0][k - 1].wait()
            for slot, device in ((0, to_tile), (1, to_branch)):
                copy = spread_copy(place, k, slot, device)
                copy.start()
                copies.append(copy)
        finish_own()
        for k in range(n):
            spread_copy(beside, k, 0, to_tile).wait_recv()
            copy = spread_copy(beside, k, 2, to_branch)
            copy.start()
            copies.append(copy)
        multiply(place)
        multiply(beside)
        for k in range(n):
            spread_copy(across, k, 1, to_branch).wait_recv()
        multiply(across)
        for k in range(n):
            spread_copy(beyond, k, 2, to_branch).wait_recv()
        multiply(beyond)
        for copy in copies:
            copy.wait_send()

    for k in range(1, n):
        source = lax.rem(me - k + n, n)
        pltpu.make_async_remote_copy(
            src_ref=outgoing_blocks.at[source],
            dst_ref=merged.at[source],
            send_sem=back_send.at[source],
            recv_sem=back_recv.at[source],
            device_id=trade_to(source),
            device_id_type=MESH,
        ).wait()

    def finish(t, _):
        found = merged[:, pl.ds(t, 1)].astype(jnp.float32).reshape(n * share, LANES)
        centred = found - jnp.mean(found, axis=0, keepdims=True)
        spread_of = jnp.mean(centred * centred, axis=0, keepdims=True)
        scaled = (centred * lax.rsqrt(spread_of + norm_eps) * out_gain[...]).astype(jnp.bfloat16)
        update = lax.dot_general(
            scaled, w_out[...], (((0,), (0,)), ((), ())), preferred_element_type=jnp.float32
        )
        for part in range(2):
            i = part * pairs + t
            gate = jax.nn.sigmoid(
                jnp.dot(normed[i], w_gate[...], preferred_element_type=jnp.float32)
            )
            out[i] = (state[i] + gate * update[part * half : (part + 1) * half]).astype(out.dtype)
        return 0

    lax.fori_loop(0, pairs, finish, 0, unroll=2)


def fused_update(
    state, flags, norm_gain, w_in, w_gate, out_gain, w_out, incoming, out_type
):
    width = w_in.shape[1] // 4
    rows, cols = flags.shape
    n = lax.axis_size("dap")
    share, pairs, half = width // n, rows // 2, rows
    normed = standardize_features(state, norm_gain, 2).astype(jnp.bfloat16)
    flags = flags.astype(jnp.float32)
    positions = jnp.transpose(normed, (1, 0, 2)) if incoming else normed
    flags = flags.T if incoming else flags
    positions = positions.reshape(2, pairs, half, width).transpose(1, 0, 2, 3)
    flags = flags.reshape(2, pairs, half).transpose(1, 0, 2).reshape(pairs, 1, LANES)
    mapped = jnp.einsum(
        "tpc,cd->tdp",
        positions.reshape(pairs, LANES, width),
        w_in,
        preferred_element_type=jnp.float32,
    )
    blocks = [mapped[:, q * width : (q + 1) * width] for q in range(4)]
    left = (jax.nn.sigmoid(blocks[1]) * blocks[0] * flags).astype(jnp.bfloat16)
    right = (jax.nn.sigmoid(blocks[3]) * blocks[2] * flags).astype(jnp.bfloat16)
    own, spread = (right, left) if incoming else (left, right)
    slots = 2 * (n - 1)
    vmem = pl.BlockSpec(memory_space=pltpu.VMEM)
    factor = (n, pairs, share, LANES)
    return pl.pallas_call(
        functools.partial(triangle_kernel, incoming),
        out_shape=jax.ShapeDtypeStruct(state.shape, out_type),
        in_specs=[vmem] * 7,
        out_specs=vmem,
        scratch_shapes=[
            pltpu.VMEM(factor, jnp.bfloat16),
            pltpu.VMEM((n, *factor), jnp.bfloat16),
            pltpu.VMEM((n * pairs * share, LANES), jnp.float32),
            pltpu.VMEM((n * pairs * share, LANES), jnp.float32),
            pltpu.VMEM((pairs * share, LANES), jnp.float32),
            pltpu.VMEM(factor, jnp.bfloat16),
            pltpu.VMEM(factor, jnp.bfloat16),
            pltpu.SemaphoreType.DMA((2, n - 1)),
            pltpu.SemaphoreType.DMA((2, n - 1)),
            pltpu.SemaphoreType.DMA((2,)),
            pltpu.SemaphoreType.DMA((slots, n)),
            pltpu.SemaphoreType.DMA((slots, n)),
            pltpu.SemaphoreType.DMA((n,)),
            pltpu.SemaphoreType.DMA((n,)),
        ],
        compiler_params=pltpu.CompilerParams(
            collective_id=1 if incoming else 0,
            has_side_effects=True,
            vmem_limit_bytes=40 * 1024 * 1024,
        ),
        cost_estimate=pl.CostEstimate(
            flops=2 * 256 * rows * cols * width, bytes_accessed=8 << 20, transcendentals=0
        ),
        name="triangle_in" if incoming else "triangle_out",
    )(own, spread, state, normed, w_gate, out_gain.reshape(width, 1), w_out)


def attention_kernel(
    heads, query, own_kv, own_bias, own_mask, out, kv, bias, mask, bias_wide, mask_wide,
    kv_send, kv_recv, bias_send, bias_recv, mask_send, mask_recv,
):
    tiles = lax.axis_size("tile")
    n, m = bias.shape[0], kv.shape[0]
    lines, sites, width = query.shape
    half = LANES // 2
    branch, tile, dap = lax.axis_index("branch"), lax.axis_index("tile"), lax.axis_index("dap")
    place = branch * tiles + tile

    def at(index):
        return {"branch": index // tiles, "tile": lax.rem(index, tiles)}

    barrier = pltpu.get_barrier_semaphore()
    for k in range(1, n):
        pl.semaphore_signal(
            barrier, inc=1, device_id={"dap": lax.rem(dap + k, n)}, device_id_type=MESH
        )
    for k in range(1, m):
        pl.semaphore_signal(
            barrier, inc=1, device_id=at(lax.rem(place + k, m)), device_id_type=MESH
        )
    pl.semaphore_wait(barrier, n + m - 2)

    across = (1 - branch) * tiles + tile
    beside = branch * tiles + (1 - tile)
    beyond = (1 - branch) * tiles + (1 - tile)
    to_tile, to_branch = at(beside), at(across)
    parts = kv_send.shape[1]
    step_lines = lines // parts

    def kv_copy(g, q, slot, device, src=None):
        piece = kv.at[g, pl.ds(q * step_lines, step_lines)]
        return pltpu.make_async_remote_copy(
            src_ref=piece if src is None else src.at[pl.ds(q * step_lines, step_lines)],
            dst_ref=piece,
            send_sem=kv_send.at[slot, q],
            recv_sem=kv_recv.at[slot, q],
            device_id=device,
            device_id_type=MESH,
        )

    waits = []
    for q in range(parts):
        for slot, device in ((0, to_tile), (1, to_branch)):
            copy = kv_copy(place, q, slot, device, own_kv)
            copy.start()
            waits.append(copy)
    small = []
    for k in range(1, m):
        small.append(
            start_remote(
                own_mask, mask.at[place], mask_send.at[k - 1], mask_recv.at[k - 1],
                at(lax.rem(place + k, m)),
            )
        )
    for k in range(1, n):
        small.append(
            start_remote(
                own_bias, bias.at[dap], bias_send.at[k - 1], bias_recv.at[k - 1],
                {"dap": lax.rem(dap + k, n)},
            )
        )
    kv[place] = own_kv[...]
    bias[dap] = own_bias[...]
    mask[place] = own_mask[...]
    for copy in small:
        copy.wait()

    for g in range(0, m, 2):
        lower = lax.broadcasted_iota(jnp.int32, (lines, LANES), 1) < half
        both = jnp.where(lower, mask[g], pltpu.roll(mask[g + 1], half, 1))
        mask_wide[:, (g // 2) * LANES : (g // 2 + 1) * LANES] = (both - 1.0) * mask_big
    for g in range(0, n, 2):
        for h in range(heads):
            first = bias[g, h].astype(jnp.float32)
            second = bias[g + 1, h].astype(jnp.float32)
            lower = lax.broadcasted_iota(jnp.int32, first.shape, 1) < half
            top = jnp.where(lower, first, pltpu.roll(second, half, 1))
            bottom = jnp.where(lower, pltpu.roll(first, half, 1), second)
            bias_wide[h * sites : (h + 1) * sites, (g // 2) * LANES : (g // 2 + 1) * LANES] = (
                jnp.concatenate([top, bottom], axis=0)
            )

    head_width = width // heads
    head_of = lax.broadcasted_iota(jnp.int32, (sites, width), 1) // head_width

    def attend(line):
        asked = query[line]
        stacked = jnp.concatenate(
            [jnp.where(head_of == h, asked, jnp.zeros_like(asked)) for h in range(heads)], axis=0
        )
        pairs = kv[:, line].reshape(m * sites, 2 * width)
        scores = lax.dot_general(
            stacked, pairs[:, :width], (((1,), (1,)), ((), ())), preferred_element_type=jnp.float32
        )
        scores = scores + bias_wide[...] + mask_wide[line : line + 1]
        weights = jnp.exp(scores - jnp.max(scores, axis=1, keepdims=True))
        row_sum = jnp.sum(weights, axis=1, keepdims=True)
        found = (
            jnp.dot(
                weights.astype(jnp.bfloat16), pairs[:, width:], preferred_element_type=jnp.float32
            )
            / row_sum
        )
        joined = jnp.zeros((sites, width), jnp.float32)
        for h in range(heads):
            joined = jnp.where(head_of == h, found[h * sites : (h + 1) * sites], joined)
        out[line] = joined

    def finish_part(q):
        kv_copy(across, q, 1, to_branch).wait_recv()
        kv_copy(beyond, q, 2, to_branch).wait_recv()
        for line in range(q * step_lines, (q + 1) * step_lines):
            attend(line)

    for q in range(parts):
        kv_copy(beside, q, 0, to_tile).wait_recv()
        copy = kv_copy(beside, q, 2, to_branch)
        copy.start()
        waits.append(copy)
        if q:
            finish_part(q - 1)
    finish_part(parts - 1)
    for copy in waits:
        copy.wait_send()


def fused_attention(query, kv, bias, mask, heads):
    lines, sites, width = query.shape
    n, m, parts = lax.axis_size("dap"), lax.axis_size(("branch", "tile")), 4
    vmem = pl.BlockSpec(memory_space=pltpu.VMEM)
    dma = pltpu.SemaphoreType.DMA
    return pl.pallas_call(
        functools.partial(attention_kernel, heads),
        out_shape=jax.ShapeDtypeStruct(query.shape, jnp.float32),
        in_specs=[vmem] * 4,
        out_specs=vmem,
        scratch_shapes=[
            pltpu.VMEM((m, *kv.shape), jnp.bfloat16),
            pltpu.VMEM((n, *bias.shape), jnp.bfloat16),
            pltpu.VMEM((m, *mask.shape), jnp.float32),
            pltpu.VMEM((heads * sites, m * sites), jnp.float32),
            pltpu.VMEM((lines, m * sites), jnp.float32),
            dma((3, parts)), dma((3, parts)),
            dma((n - 1,)), dma((n - 1,)), dma((m - 1,)), dma((m - 1,)),
        ],
        compiler_params=pltpu.CompilerParams(
            collective_id=2, has_side_effects=True, vmem_limit_bytes=32 * 1024 * 1024
        ),
        cost_estimate=pl.CostEstimate(
            flops=4 * lines * heads * sites * m * sites * width,
            bytes_accessed=4 << 20,
            transcendentals=lines * heads * sites * m * sites,
        ),
        name="attention",
    )(query, kv, bias, mask)


def factor_kernel(
    left, right, left_all, right_all, left_got, right_got,
    left_send, left_recv, right_send, right_recv,
):
    tiles = lax.axis_size("tile")
    n = left_got.shape[0]
    dap = lax.axis_index("dap")
    block = lax.axis_index("branch") * tiles + lax.axis_index("tile")

    def at(index, column):
        return {"branch": index // tiles, "tile": lax.rem(index, tiles), "dap": column}

    def others(index, column):
        return jnp.logical_or(index != block, column != dap)

    barrier = pltpu.get_barrier_semaphore()
    for k in range(1, n * n):
        peer = lax.rem(block * n + dap + k, n * n)
        pl.semaphore_signal(
            barrier, inc=1, device_id=at(peer // n, lax.rem(peer, n)), device_id_type=MESH
        )
    pl.semaphore_wait(barrier, n * n - 1)

    copies = [
        start_remote(
            left, left_got.at[dap], left_send.at[k - 1], left_recv.at[k - 1],
            {"dap": lax.rem(dap + k, n)},
        )
        for k in range(1, n)
    ]

    def right_copy(slot, index, column, k):
        return pltpu.make_async_remote_copy(
            src_ref=right,
            dst_ref=right_got.at[slot],
            send_sem=right_send.at[k],
            recv_sem=right_recv.at[slot],
            device_id=at(index, column),
            device_id_type=MESH,
        )

    for k in range(n):

        @pl.when(others(k, block))
        def _(k=k):
            right_copy(dap, k, block, k).start()

    left_got[dap] = left[...]

    @pl.when(dap == block)
    def _():
        right_got[dap] = right[...]

    for copy in copies:
        copy.wait()
    for k in range(n):

        @pl.when(others(dap, k))
        def _(k=k):
            right_copy(k, dap, k, k).wait_recv()

        @pl.when(others(k, block))
        def _(k=k):
            right_copy(dap, k, block, k).wait_send()

    left_all[...] = left_got[...]
    right_all[...] = right_got[...]


def trade_factors(left, right):
    n = lax.axis_size("dap")
    vmem = pl.BlockSpec(memory_space=pltpu.VMEM)
    dma = pltpu.SemaphoreType.DMA
    shape = (n, *left.shape)
    return pl.pallas_call(
        factor_kernel,
        out_shape=[jax.ShapeDtypeStruct(shape, jnp.bfloat16)] * 2,
        in_specs=[vmem] * 2,
        out_specs=[vmem] * 2,
        scratch_shapes=[
            pltpu.VMEM(shape, jnp.bfloat16),
            pltpu.VMEM(shape, jnp.bfloat16),
            dma((n - 1,)), dma((n - 1,)), dma((n,)), dma((n,)),
        ],
        compiler_params=pltpu.CompilerParams(collective_id=3, has_side_effects=True),
        cost_estimate=pl.CostEstimate(flops=0, bytes_accessed=1 << 20, transcendentals=0),
        name="factors",
    )(left, right)


def body(
    homolog_hidden,
    duo_hidden,
    homolog_valid_flags,
    duo_valid_flags,
    polymer_labeling,
    monomer_serials,
    separation_bin_vectors,
    duo_logit_rescale,
    duo_logit_projector,
    homolog_heeded_rescale,
    qkv_valve_projectors,
    heeded_exit_projector,
    dyadic_rescale,
    dyadic_factor_projector,
    dyadic_exit_projector,
    triad_entry_rescales,
    triad_entry_projectors,
    triad_valve_projectors,
    triad_exit_rescales,
    triad_exit_projectors,
):
    lines_each_shard, sites_each_shard, lineup_feature_extent = homolog_hidden.shape
    columns_per_device = duo_hidden.shape[1]
    number_of_heads = duo_logit_projector.shape[1]
    square = (
        duo_hidden.shape[:2] == (LANES // 2, LANES // 2)
        and lax.axis_size("branch") == lax.axis_size("tile") == 2
        and lax.axis_size("dap") == 4
    )
    head_channels = lineup_feature_extent // number_of_heads
    outer_channels = dyadic_factor_projector.shape[1] // 2
    row_start = lax.axis_index(("branch", "tile")) * sites_each_shard
    col_start = lax.axis_index("dap") * columns_per_device
    rel_reach = (REL_BINS - 2) // 2
    res_rows = lax.dynamic_slice_in_dim(monomer_serials, row_start, sites_each_shard)
    res_cols = lax.dynamic_slice_in_dim(monomer_serials, col_start, columns_per_device)
    chain_rows = lax.dynamic_slice_in_dim(polymer_labeling, row_start, sites_each_shard)
    chain_cols = lax.dynamic_slice_in_dim(polymer_labeling, col_start, columns_per_device)
    offset = jnp.clip(res_rows[:, None] - res_cols[None, :], -rel_reach, rel_reach) + rel_reach
    rel_bins = jnp.where(chain_rows[:, None] == chain_cols[None, :], offset, REL_BINS - 1)
    one_hot = (rel_bins[:, :, None] == jnp.arange(REL_BINS, dtype=jnp.int32)[None, None, :]).astype(
        jnp.bfloat16
    )
    duo_hidden_values = duo_hidden.astype(jnp.float32) + jnp.einsum(
        "ijb,bc->ijc", one_hot, separation_bin_vectors, preferred_element_type=jnp.float32
    )
    pair_normed = standardize_features(duo_hidden_values, duo_logit_rescale, 2).astype(jnp.bfloat16)
    lineup_standardized = standardize_features(homolog_hidden, homolog_heeded_rescale, 2).astype(
        jnp.bfloat16
    )
    mapped_contents = jnp.einsum(
        "ezp,pb->ezb", lineup_standardized, qkv_valve_projectors, preferred_element_type=jnp.float32
    )
    asking_array = (mapped_contents[..., :lineup_feature_extent] * head_channels ** (-0.5)).astype(
        jnp.bfloat16
    )
    asking_array = asking_array.reshape(
        lines_each_shard, sites_each_shard, number_of_heads, head_channels
    )
    key_value_pairs = mapped_contents[
        ..., lineup_feature_extent : 3 * lineup_feature_extent
    ].astype(jnp.bfloat16)
    sigmoid_switches = jax.nn.sigmoid(mapped_contents[..., 3 * lineup_feature_extent :])
    if square:
        pairs = sites_each_shard // 2
        pair_order = pair_normed.reshape(2, pairs, columns_per_device, -1).transpose(1, 0, 2, 3)
        local_bias = jnp.einsum(
            "tpc,ch->htp",
            pair_order.reshape(pairs, LANES, -1),
            duo_logit_projector,
            preferred_element_type=jnp.float32,
        ).astype(jnp.bfloat16)
        focused_readout = fused_attention(
            asking_array.reshape(homolog_hidden.shape),
            key_value_pairs,
            local_bias,
            jnp.pad(
                homolog_valid_flags.astype(jnp.float32), ((0, 0), (0, LANES - sites_each_shard))
            ),
            number_of_heads,
        )
    else:
        local_bias = jnp.einsum(
            "ijc,ch->hij", pair_normed, duo_logit_projector, preferred_element_type=jnp.float32
        ).astype(jnp.bfloat16)
        row_bias = lax.all_gather(
            local_bias.reshape(number_of_heads, sites_each_shard * columns_per_device), "dap", axis=0
        ).reshape(-1, number_of_heads, sites_each_shard, columns_per_device)
        row_bias = jnp.transpose(row_bias, (1, 2, 0, 3)).reshape(number_of_heads, sites_each_shard, -1)
        mask_grid = lax.all_gather(
            homolog_valid_flags.astype(jnp.bfloat16), ("dap", "branch", "tile"), axis=0
        ).reshape(lax.axis_size("dap"), -1, lines_each_shard, sites_each_shard)
        mask_grid = jnp.transpose(mask_grid, (0, 2, 1, 3)).reshape(
            lax.axis_size("dap") * lines_each_shard, -1
        )
        run_max = jnp.full((lines_each_shard, number_of_heads, sites_each_shard), -jnp.inf, jnp.float32)
        run_sum = jnp.zeros((lines_each_shard, number_of_heads, sites_each_shard), jnp.float32)
        run_acc = jnp.zeros(
            (lines_each_shard, number_of_heads, sites_each_shard, head_channels), jnp.float32
        )
        key_value_slice = lax.all_gather(key_value_pairs, ("branch", "tile"), axis=1, tiled=True)
        mask_piece = lax.dynamic_slice_in_dim(
            mask_grid, lax.axis_index("dap") * lines_each_shard, lines_each_shard, axis=0
        )
        slice_length = key_value_slice.shape[1]
        key_per_head = key_value_slice[..., :lineup_feature_extent].reshape(
            lines_each_shard, slice_length, number_of_heads, head_channels
        )
        value_per_head = key_value_slice[..., lineup_feature_extent:].reshape(
            lines_each_shard, slice_length, number_of_heads, head_channels
        )
        key_bias = row_bias.astype(jnp.float32)
        scores = jnp.einsum(
            "sihd,sjhd->shij", asking_array, key_per_head, preferred_element_type=jnp.float32
        )
        scores = (
            scores
            + key_bias[None]
            + ((mask_piece.astype(jnp.float32) - 1.0) * mask_big)[:, None, None, :]
        )
        new_max = jnp.max(scores, axis=-1)
        old_scale = jnp.exp(run_max - new_max)
        weights = jnp.exp(scores - new_max[..., None])
        run_sum = run_sum * old_scale + jnp.sum(weights, axis=-1)
        run_acc = run_acc * old_scale[..., None] + jnp.einsum(
            "shij,sjhd->shid",
            weights.astype(jnp.bfloat16),
            value_per_head,
            preferred_element_type=jnp.float32,
        )
        run_max, run_sum, run_acc = (new_max, run_sum, run_acc)
        focused_readout = run_acc / run_sum[..., None]
        focused_readout = jnp.transpose(focused_readout, (0, 2, 1, 3)).reshape(
            lines_each_shard, sites_each_shard, lineup_feature_extent
        )
    merged_focus_groups = (sigmoid_switches * focused_readout).astype(jnp.bfloat16)
    lineup_updated_state = (
        homolog_hidden.astype(jnp.float32)
        + jnp.einsum(
            "ezp,pb->ezb",
            merged_focus_groups,
            heeded_exit_projector,
            preferred_element_type=jnp.float32,
        )
    ).astype(jnp.bfloat16)
    outer_product_normalized = standardize_features(lineup_updated_state, dyadic_rescale, 2).astype(
        jnp.bfloat16
    )
    exit_by_channel = dyadic_exit_projector.reshape(outer_channels, outer_channels, -1)
    if square:
        flag_row = homolog_valid_flags.reshape(1, -1).astype(jnp.float32)
        factors = (
            jnp.einsum(
                "ep,pb->be",
                outer_product_normalized.reshape(-1, lineup_feature_extent),
                dyadic_factor_projector,
                preferred_element_type=jnp.float32,
            )
            * flag_row
        ).astype(jnp.bfloat16)
        flag_rows = jnp.broadcast_to(flag_row, (16, flag_row.shape[1])).astype(jnp.bfloat16)
        traded = trade_factors(
            jnp.concatenate([factors[:outer_channels], flag_rows]),
            jnp.concatenate([factors[outer_channels:], flag_rows]),
        )
        left_rows, right_rows = (
            part[:, :outer_channels].reshape(
                -1, outer_channels, lines_each_shard, sites_each_shard
            )
            for part in traded
        )
        mask_rows, mask_right = (
            part[:, outer_channels].reshape(-1, sites_each_shard) for part in traded
        )
        counts = jnp.einsum("si,sj->ij", mask_rows, mask_right, preferred_element_type=jnp.float32)
        spread_right = jnp.einsum(
            "gdsj,cdz->gscjz", right_rows, exit_by_channel, preferred_element_type=jnp.float32
        ).astype(jnp.bfloat16)
        update = jnp.einsum(
            "gcsi,gscjz->ijz", left_rows, spread_right, preferred_element_type=jnp.float32
        )
    else:
        factors = (
            jnp.einsum(
                "ezp,pb->ezb",
                outer_product_normalized,
                dyadic_factor_projector,
                preferred_element_type=jnp.float32,
            )
            * homolog_valid_flags.astype(jnp.float32)[..., None]
        )
        factors = factors.astype(jnp.bfloat16)
        all_factors = lax.all_gather(factors, ("dap", "branch", "tile"), axis=0).reshape(
            lax.axis_size("dap"), -1, lines_each_shard, sites_each_shard, 2 * outer_channels
        )
        alignment_rows = mask_grid.shape[0]
        left_rows = lax.dynamic_index_in_dim(
            all_factors, lax.axis_index(("branch", "tile")), axis=1, keepdims=False
        )[..., :outer_channels].reshape(alignment_rows, sites_each_shard, outer_channels)
        block = col_start // sites_each_shard
        right_rows = lax.dynamic_index_in_dim(all_factors, block, axis=1, keepdims=False)[
            ..., outer_channels:
        ].reshape(alignment_rows, sites_each_shard, outer_channels)
        right_rows = lax.dynamic_slice_in_dim(
            right_rows, col_start - block * sites_each_shard, columns_per_device, axis=1
        )
        mask_rows = lax.dynamic_slice_in_dim(mask_grid, row_start, sites_each_shard, axis=1)
        mask_right = lax.dynamic_slice_in_dim(mask_grid, col_start, columns_per_device, axis=1)
        counts = jnp.einsum("si,sj->ij", mask_rows, mask_right, preferred_element_type=jnp.float32)
        spread_right = jnp.einsum(
            "sjd,cdz->scjz", right_rows, exit_by_channel, preferred_element_type=jnp.float32
        ).astype(jnp.bfloat16)
        update = jnp.einsum(
            "sic,scjz->ijz", left_rows, spread_right, preferred_element_type=jnp.float32
        )
    duo_hidden_values = duo_hidden_values + update / (count_eps + counts)[..., None]
    for threefold_module in range(2):
        parameters = (
            triad_entry_rescales[threefold_module],
            triad_entry_projectors[threefold_module],
            triad_valve_projectors[threefold_module],
            triad_exit_rescales[threefold_module],
            triad_exit_projectors[threefold_module],
            threefold_module == 1,
        )
        if square:
            out_type = jnp.bfloat16 if threefold_module == 1 else jnp.float32
            duo_hidden_values = fused_update(
                duo_hidden_values, duo_valid_flags, *parameters, out_type
            )
        else:
            duo_hidden_values = threeway_update(duo_hidden_values, duo_valid_flags, *parameters)
    return (lineup_updated_state, duo_hidden_values.astype(jnp.bfloat16))


def solution(mesh):
    placed = (
        P(("groups", "dap"), ("branch", "tile"), None),
        P(("groups", "branch", "tile"), "dap", None),
        P(("groups", "dap"), ("branch", "tile")),
        P(("groups", "branch", "tile"), "dap"),
        P("groups"),
        P("groups"),
        P(),
        P(),
        P(),
        P(),
        P(),
        P(),
        P(),
        P(),
        P(),
        P(),
        P(),
        P(),
        P(),
        P(),
    )
    return jax.shard_map(
        body,
        mesh=mesh,
        in_specs=placed,
        out_specs=(
            P(("groups", "dap"), ("branch", "tile"), None),
            P(("groups", "branch", "tile"), "dap", None),
        ),
        check_vma=False,
    )
```

```python
import functools

import jax
import jax.numpy as jnp
from jax import lax
from jax.experimental import pallas as pl
from jax.experimental.pallas import tpu as pltpu
from jax.sharding import PartitionSpec as P

REL_BINS = 66


norm_eps = 1e-05
mask_big = 1000000000.0
count_eps = 0.001


def standardize_features(values, norm_gain, norm_axis):
    values = values.astype(jnp.float32)
    mean_val = jnp.mean(values, axis=norm_axis, keepdims=True)
    centred = values - mean_val
    spread = jnp.mean(centred * centred, axis=norm_axis, keepdims=True)
    return centred * lax.rsqrt(spread + norm_eps) * norm_gain


def threeway_update(
    duo_hidden_values, duo_valid_flags, norm_gain, w_in, w_gate, out_gain, w_out, incoming
):
    width_tri = w_in.shape[1] // 4
    rows, cols = duo_valid_flags.shape
    tri_normed = standardize_features(duo_hidden_values, norm_gain, 2).astype(jnp.bfloat16)
    flags = duo_valid_flags.astype(jnp.float32)
    if incoming:
        positions = jnp.transpose(tri_normed, (1, 0, 2))
        flags = flags.T
        share_axis, spread_axis = ("branch", "tile"), "dap"
        kept, summed = cols, rows
    else:
        positions = tri_normed
        share_axis, spread_axis = "dap", ("branch", "tile")
        kept, summed = rows, cols
    positions = positions.reshape(kept * summed, width_tri)
    flags = flags.reshape(1, kept * summed)
    shares = lax.axis_size(share_axis)
    share = width_tri // shares
    mapped = jnp.einsum("pc,cd->dp", positions, w_in, preferred_element_type=jnp.float32)
    blocks = [mapped[n * width_tri : (n + 1) * width_tri] for n in range(4)]
    left_fac = (jax.nn.sigmoid(blocks[1]) * blocks[0] * flags).astype(jnp.bfloat16)
    right_fac = (jax.nn.sigmoid(blocks[3]) * blocks[2] * flags).astype(jnp.bfloat16)

    def by_channel_share(factor):
        got = lax.all_to_all(
            factor.reshape(shares, share, kept * summed), share_axis, split_axis=0, concat_axis=0
        )
        got = got.reshape(shares, share, kept, summed)
        return jnp.transpose(got, (1, 2, 0, 3)).reshape(share, kept, shares * summed)

    if incoming:
        left_own = by_channel_share(left_fac)
        left_all = lax.all_gather(left_own, spread_axis, axis=0)
        right_own = by_channel_share(right_fac)
        product = jnp.einsum(
            "gcik,cjk->gicj", left_all, right_own, preferred_element_type=jnp.float32
        ).astype(jnp.bfloat16)
        product = product.reshape(shares, rows, share, cols)
        product = jnp.transpose(product, (0, 2, 1, 3))
    else:
        right_own = by_channel_share(right_fac)
        right_all = lax.all_gather(right_own, spread_axis, axis=0)
        left_own = by_channel_share(left_fac)
        product = jnp.einsum(
            "cik,gcjk->gjci", left_own, right_all, preferred_element_type=jnp.float32
        ).astype(jnp.bfloat16)
        product = product.reshape(shares, cols, share, rows)
        product = jnp.transpose(product, (0, 2, 3, 1))
    merged = lax.all_to_all(
        product.reshape(shares, share, rows * cols), share_axis, split_axis=0, concat_axis=0
    ).reshape(width_tri, rows * cols)
    sigmoid_switches = jax.nn.sigmoid(
        jnp.einsum("ijc,cd->ijd", tri_normed, w_gate, preferred_element_type=jnp.float32)
    )
    product_normed = standardize_features(merged, out_gain[:, None], 0).astype(jnp.bfloat16)
    update = jnp.einsum("cp,cz->pz", product_normed, w_out, preferred_element_type=jnp.float32)
    return duo_hidden_values + sigmoid_switches * update.reshape(rows, cols, width_tri)


MESH = pl.DeviceIdType.MESH
LANES = 128


def start_remote(src, dst, send_sem, recv_sem, device):
    copy = pltpu.make_async_remote_copy(
        src_ref=src,
        dst_ref=dst,
        send_sem=send_sem,
        recv_sem=recv_sem,
        device_id=device,
        device_id_type=MESH,
    )
    copy.start()
    return copy


def triangle_kernel(
    incoming,
    state,
    flags,
    norm_gain,
    w_own,
    w_spread,
    w_gate,
    out_gain,
    w_out,
    out,
    own_in,
    spread_in,
    normed,
    own,
    spread,
    own_wide,
    spread_wide,
    product_wide,
    outgoing_blocks,
    merged,
    trade_send,
    trade_recv,
    local_sem,
    spread_send,
    spread_recv,
    back_send,
    back_recv,
):
    n, pairs, share = own.shape[0], own.shape[1], own.shape[2]
    m = spread.shape[0]
    half = LANES // 2
    tiles = lax.axis_size("tile")
    branch, tile, dap = lax.axis_index("branch"), lax.axis_index("tile"), lax.axis_index("dap")
    block = branch * tiles + tile

    def by_block(index):
        return {"branch": index // tiles, "tile": lax.rem(index, tiles)}

    def by_dap(index):
        return {"dap": index}

    if incoming:
        me, trade_to, place, spread_to = block, by_block, dap, by_dap
    else:
        me, trade_to, place, spread_to = dap, by_dap, block, by_block

    barrier = pltpu.get_barrier_semaphore()
    for k in range(1, n):
        pl.semaphore_signal(
            barrier, inc=1, device_id=trade_to(lax.rem(me + k, n)), device_id_type=MESH
        )
    for k in range(1, m):
        pl.semaphore_signal(
            barrier, inc=1, device_id=spread_to(lax.rem(place + k, m)), device_id_type=MESH
        )
    rows, cols, width = state.shape

    def normalise(i, _):
        values = state[i]
        centred = values - jnp.mean(values, axis=1, keepdims=True)
        spread_of = jnp.mean(centred * centred, axis=1, keepdims=True)
        normed[pl.ds(pl.multiple_of(i * cols, cols), cols), :] = (
            centred * lax.rsqrt(spread_of + norm_eps) * norm_gain[...]
        )
        return 0

    lax.fori_loop(0, rows, normalise, 0, unroll=4)

    def project(weights, factor):
        def step(t, _):
            if incoming:
                chosen = [normed[pl.ds(t + part * pairs, rows, stride=cols), :] for part in (0, 1)]
            else:
                chosen = [
                    normed[pl.ds(pl.multiple_of((t + part * pairs) * cols, cols), cols), :]
                    for part in (0, 1)
                ]
            mapped = lax.dot_general(
                weights[...],
                jnp.concatenate(chosen, axis=0).astype(jnp.bfloat16),
                (((1,), (1,)), ((), ())),
                preferred_element_type=jnp.float32,
            )
            factor[t] = (jax.nn.sigmoid(mapped[width:]) * mapped[:width] * flags[t]).astype(
                jnp.bfloat16
            )
            return 0

        lax.fori_loop(0, pairs, step, 0, unroll=2)

    def channels(ref, index):
        return ref.at[:, pl.ds(pl.multiple_of(index * share, share), share), :]

    trades = [[], []]
    plans = ((w_spread, spread_in, spread.at[place, me]), (w_own, own_in, own.at[me]))
    for which, (weights, src, dst) in enumerate(plans):
        project(weights, src)
        if which == 0:
            pl.semaphore_wait(barrier, n + m - 2)
        for k in range(1, n):
            to = lax.rem(me + k, n)
            trades[which].append(
                start_remote(
                    channels(src, to),
                    dst,
                    trade_send.at[which, k - 1],
                    trade_recv.at[which, k - 1],
                    trade_to(to),
                )
            )
    locals_ = [
        pltpu.make_async_copy(channels(spread_in, me), spread.at[place, me], local_sem.at[0]),
        pltpu.make_async_copy(channels(own_in, me), own.at[me], local_sem.at[1]),
    ]
    for copy in locals_:
        copy.start()

    def widen(dst, load):
        def step(s, _):
            dst[pl.ds(pl.multiple_of(s * pairs * share, share), pairs * share), :] = (
                load(s).astype(jnp.float32).reshape(pairs * share, LANES)
            )
            return 0

        lax.fori_loop(0, n, step, 0)

    def matrix(ref, c):
        lower = lax.broadcasted_iota(jnp.int32, (pairs, LANES), 1) < half
        columns = []
        for s in range(0, n, 2):
            first = ref[pl.ds(s * pairs * share + c, pairs, stride=share), :]
            second = ref[pl.ds((s + 1) * pairs * share + c, pairs, stride=share), :]
            top = jnp.where(lower, first, pltpu.roll(second, half, 1))
            bottom = jnp.where(lower, pltpu.roll(first, half, 1), second)
            columns.append(jnp.concatenate([top, bottom], axis=0))
        return jnp.concatenate(columns, axis=1).astype(jnp.bfloat16)

    def multiply(g):
        widen(spread_wide, lambda s: spread[g, s])

        def step(c, _):
            mine, other = matrix(own_wide, c), matrix(spread_wide, c)
            left, right = (other, mine) if incoming else (mine, other)
            found = lax.dot_general(
                left, right, (((1,), (1,)), ((), ())), preferred_element_type=jnp.float32
            )
            product_wide[pl.ds(c, pairs, stride=share), :] = jnp.concatenate(
                [found[:pairs], found[pairs:]], axis=1
            )
            return 0

        lax.fori_loop(0, share, step, 0, unroll=4)
        outgoing_blocks[g] = (
            product_wide[...].reshape(pairs, share, LANES).astype(jnp.bfloat16)
        )

        @pl.when(g != me)
        def _():
            start_remote(
                outgoing_blocks.at[g],
                merged.at[me],
                back_send.at[g],
                back_recv.at[me],
                trade_to(g),
            )

        @pl.when(g == me)
        def _():
            merged[g] = outgoing_blocks[g]

    def spread_copy(g, k, slot, device):
        piece = spread.at[g, lax.rem(me - k + n, n)]
        return pltpu.make_async_remote_copy(
            src_ref=piece,
            dst_ref=piece,
            send_sem=spread_send.at[slot, k],
            recv_sem=spread_recv.at[slot, k],
            device_id=device,
            device_id_type=MESH,
        )

    def finish_own():
        locals_[1].wait()
        for copy in trades[1]:
            copy.wait()
        widen(own_wide, lambda s: own[s])

    if incoming:
        right, left = place + 1, place - 1
        has_right, has_left = right < m, left >= 0
        sides = ((0, 1, right, has_right), (1, -1, left, has_left))
        for k in range(n):
            if k == 0:
                locals_[0].wait()
            else:
                trades[0][k - 1].wait()
            for side, _, to, there in sides:

                @pl.when(there)
                def _(side=side, to=to, k=k):
                    spread_copy(place, k, side * (m - 1), spread_to(to)).start()

        finish_own()
        multiply(place)
        for h in range(1, m):
            for k in range(n):
                for side, sign, to, there in sides:
                    g = place - sign * h
                    has_block = (g >= 0) if sign > 0 else (g < m)

                    @pl.when(has_block)
                    def _(side=side, to=to, there=there, g=g, h=h, k=k):
                        spread_copy(
                            g, k, side * (m - 1) + h - 1, spread_to(lax.rem(place + 1, m))
                        ).wait_recv()
                        if h < m - 1:

                            @pl.when(there)
                            def _():
                                spread_copy(g, k, side * (m - 1) + h, spread_to(to)).start()

            for side, sign, to, there in sides:
                g = place - sign * h
                has_block = (g >= 0) if sign > 0 else (g < m)

                @pl.when(has_block)
                def _(g=g):
                    multiply(g)

        for side, sign, to, there in sides:
            for h in range(m - 1):
                g = place - sign * h
                has_block = (g >= 0) if sign > 0 else (g < m)

                @pl.when(jnp.logical_and(there, has_block))
                def _(side=side, g=g, h=h, to=to):
                    for k in range(n):
                        spread_copy(g, k, side * (m - 1) + h, spread_to(to)).wait_send()

    else:
        across = (1 - branch) * tiles + tile
        beside = branch * tiles + (1 - tile)
        beyond = (1 - branch) * tiles + (1 - tile)
        to_tile, to_branch = spread_to(beside), spread_to(across)
        copies = []
        for k in range(n):
            if k == 0:
                locals_[0].wait()
            else:
                trades[0][k - 1].wait()
            for slot, device in ((0, to_tile), (1, to_branch)):
                copy = spread_copy(place, k, slot, device)
                copy.start()
                copies.append(copy)
        finish_own()
        for k in range(n):
            spread_copy(beside, k, 0, to_tile).wait_recv()
            copy = spread_copy(beside, k, 2, to_branch)
            copy.start()
            copies.append(copy)
        multiply(place)
        multiply(beside)
        for k in range(n):
            spread_copy(across, k, 1, to_branch).wait_recv()
        multiply(across)
        for k in range(n):
            spread_copy(beyond, k, 2, to_branch).wait_recv()
        multiply(beyond)
        for copy in copies:
            copy.wait_send()

    for k in range(1, n):
        source = lax.rem(me - k + n, n)
        pltpu.make_async_remote_copy(
            src_ref=outgoing_blocks.at[source],
            dst_ref=merged.at[source],
            send_sem=back_send.at[source],
            recv_sem=back_recv.at[source],
            device_id=trade_to(source),
            device_id_type=MESH,
        ).wait()

    def finish(t, _):
        found = merged[:, pl.ds(t, 1)].astype(jnp.float32).reshape(n * share, LANES)
        centred = found - jnp.mean(found, axis=0, keepdims=True)
        spread_of = jnp.mean(centred * centred, axis=0, keepdims=True)
        scaled = (centred * lax.rsqrt(spread_of + norm_eps) * out_gain[...]).astype(jnp.bfloat16)
        update = lax.dot_general(
            scaled, w_out[...], (((0,), (0,)), ((), ())), preferred_element_type=jnp.float32
        )
        for part in range(2):
            i = part * pairs + t
            gate = jax.nn.sigmoid(
                jnp.dot(
                    normed[pl.ds(pl.multiple_of(i * cols, cols), cols), :].astype(jnp.bfloat16),
                    w_gate[...],
                    preferred_element_type=jnp.float32,
                )
            )
            out[i] = (state[i] + gate * update[part * half : (part + 1) * half]).astype(out.dtype)
        return 0

    lax.fori_loop(0, pairs, finish, 0, unroll=2)


def fused_update(
    state, flags, norm_gain, w_in, w_gate, out_gain, w_out, incoming, out_type
):
    width = w_in.shape[1] // 4
    rows, cols = flags.shape
    n = lax.axis_size("dap")
    share, pairs = width // n, rows // 2
    flags = flags.astype(jnp.float32)
    flags = (flags.T if incoming else flags).reshape(2, pairs, -1)
    flags = flags.transpose(1, 0, 2).reshape(pairs, 1, LANES)
    turned = w_in.T
    left, right = turned[: 2 * width], turned[2 * width :]
    own, spread = (right, left) if incoming else (left, right)
    slots = 2 * (n - 1)
    vmem = pl.BlockSpec(memory_space=pltpu.VMEM)
    factor = (n, pairs, share, LANES)
    return pl.pallas_call(
        functools.partial(triangle_kernel, incoming),
        out_shape=jax.ShapeDtypeStruct(state.shape, out_type),
        in_specs=[vmem] * 8,
        out_specs=vmem,
        scratch_shapes=[
            pltpu.VMEM((pairs, width, LANES), jnp.bfloat16),
            pltpu.VMEM((pairs, width, LANES), jnp.bfloat16),
            pltpu.VMEM((rows * cols, width), jnp.float32),
            pltpu.VMEM(factor, jnp.bfloat16),
            pltpu.VMEM((n, *factor), jnp.bfloat16),
            pltpu.VMEM((n * pairs * share, LANES), jnp.float32),
            pltpu.VMEM((n * pairs * share, LANES), jnp.float32),
            pltpu.VMEM((pairs * share, LANES), jnp.float32),
            pltpu.VMEM(factor, jnp.bfloat16),
            pltpu.VMEM(factor, jnp.bfloat16),
            pltpu.SemaphoreType.DMA((2, n - 1)),
            pltpu.SemaphoreType.DMA((2, n - 1)),
            pltpu.SemaphoreType.DMA((2,)),
            pltpu.SemaphoreType.DMA((slots, n)),
            pltpu.SemaphoreType.DMA((slots, n)),
            pltpu.SemaphoreType.DMA((n,)),
            pltpu.SemaphoreType.DMA((n,)),
        ],
        compiler_params=pltpu.CompilerParams(
            collective_id=1 if incoming else 0,
            has_side_effects=True,
            vmem_limit_bytes=40 * 1024 * 1024,
        ),
        cost_estimate=pl.CostEstimate(
            flops=2 * 256 * rows * cols * width, bytes_accessed=8 << 20, transcendentals=0
        ),
        name="triangle_in" if incoming else "triangle_out",
    )(
        state,
        flags,
        norm_gain.reshape(1, width),
        own,
        spread,
        w_gate,
        out_gain.reshape(width, 1),
        w_out,
    )


def attention_kernel(
    heads, query, own_kv, own_bias, own_mask, out, kv, bias, mask, bias_wide, mask_wide,
    kv_send, kv_recv, bias_send, bias_recv, mask_send, mask_recv,
):
    tiles = lax.axis_size("tile")
    n, m = bias.shape[0], kv.shape[0]
    lines, sites, width = query.shape
    half = LANES // 2
    branch, tile, dap = lax.axis_index("branch"), lax.axis_index("tile"), lax.axis_index("dap")
    place = branch * tiles + tile

    def at(index):
        return {"branch": index // tiles, "tile": lax.rem(index, tiles)}

    barrier = pltpu.get_barrier_semaphore()
    for k in range(1, n):
        pl.semaphore_signal(
            barrier, inc=1, device_id={"dap": lax.rem(dap + k, n)}, device_id_type=MESH
        )
    for k in range(1, m):
        pl.semaphore_signal(
            barrier, inc=1, device_id=at(lax.rem(place + k, m)), device_id_type=MESH
        )
    pl.semaphore_wait(barrier, n + m - 2)

    across = (1 - branch) * tiles + tile
    beside = branch * tiles + (1 - tile)
    beyond = (1 - branch) * tiles + (1 - tile)
    to_tile, to_branch = at(beside), at(across)
    parts = kv_send.shape[1]
    step_lines = lines // parts

    def kv_copy(g, q, slot, device, src=None):
        piece = kv.at[g, pl.ds(q * step_lines, step_lines)]
        return pltpu.make_async_remote_copy(
            src_ref=piece if src is None else src.at[pl.ds(q * step_lines, step_lines)],
            dst_ref=piece,
            send_sem=kv_send.at[slot, q],
            recv_sem=kv_recv.at[slot, q],
            device_id=device,
            device_id_type=MESH,
        )

    waits = []
    for q in range(parts):
        for slot, device in ((0, to_tile), (1, to_branch)):
            copy = kv_copy(place, q, slot, device, own_kv)
            copy.start()
            waits.append(copy)
    small = []
    for k in range(1, m):
        small.append(
            start_remote(
                own_mask, mask.at[place], mask_send.at[k - 1], mask_recv.at[k - 1],
                at(lax.rem(place + k, m)),
            )
        )
    for k in range(1, n):
        small.append(
            start_remote(
                own_bias, bias.at[dap], bias_send.at[k - 1], bias_recv.at[k - 1],
                {"dap": lax.rem(dap + k, n)},
            )
        )
    kv[place] = own_kv[...]
    bias[dap] = own_bias[...]
    mask[place] = own_mask[...]
    for copy in small:
        copy.wait()

    for g in range(0, m, 2):
        lower = lax.broadcasted_iota(jnp.int32, (lines, LANES), 1) < half
        both = jnp.where(lower, mask[g], pltpu.roll(mask[g + 1], half, 1))
        mask_wide[:, (g // 2) * LANES : (g // 2 + 1) * LANES] = (both - 1.0) * mask_big
    for g in range(0, n, 2):
        for h in range(heads):
            first = bias[g, h].astype(jnp.float32)
            second = bias[g + 1, h].astype(jnp.float32)
            lower = lax.broadcasted_iota(jnp.int32, first.shape, 1) < half
            top = jnp.where(lower, first, pltpu.roll(second, half, 1))
            bottom = jnp.where(lower, pltpu.roll(first, half, 1), second)
            bias_wide[h * sites : (h + 1) * sites, (g // 2) * LANES : (g // 2 + 1) * LANES] = (
                jnp.concatenate([top, bottom], axis=0)
            )

    head_width = width // heads
    head_of = lax.broadcasted_iota(jnp.int32, (sites, width), 1) // head_width

    def attend(line):
        asked = query[line]
        stacked = jnp.concatenate(
            [jnp.where(head_of == h, asked, jnp.zeros_like(asked)) for h in range(heads)], axis=0
        )
        pairs = kv[:, line].reshape(m * sites, 2 * width)
        scores = lax.dot_general(
            stacked, pairs[:, :width], (((1,), (1,)), ((), ())), preferred_element_type=jnp.float32
        )
        scores = scores + bias_wide[...] + mask_wide[line : line + 1]
        weights = jnp.exp(scores - jnp.max(scores, axis=1, keepdims=True))
        row_sum = jnp.sum(weights, axis=1, keepdims=True)
        found = (
            jnp.dot(
                weights.astype(jnp.bfloat16), pairs[:, width:], preferred_element_type=jnp.float32
            )
            / row_sum
        )
        joined = jnp.zeros((sites, width), jnp.float32)
        for h in range(heads):
            joined = jnp.where(head_of == h, found[h * sites : (h + 1) * sites], joined)
        out[line] = joined

    def finish_part(q):
        kv_copy(across, q, 1, to_branch).wait_recv()
        kv_copy(beyond, q, 2, to_branch).wait_recv()
        for line in range(q * step_lines, (q + 1) * step_lines):
            attend(line)

    for q in range(parts):
        kv_copy(beside, q, 0, to_tile).wait_recv()
        copy = kv_copy(beside, q, 2, to_branch)
        copy.start()
        waits.append(copy)
        if q:
            finish_part(q - 1)
    finish_part(parts - 1)
    for copy in waits:
        copy.wait_send()


def fused_attention(query, kv, bias, mask, heads):
    lines, sites, width = query.shape
    n, m, parts = lax.axis_size("dap"), lax.axis_size(("branch", "tile")), 4
    vmem = pl.BlockSpec(memory_space=pltpu.VMEM)
    dma = pltpu.SemaphoreType.DMA
    return pl.pallas_call(
        functools.partial(attention_kernel, heads),
        out_shape=jax.ShapeDtypeStruct(query.shape, jnp.float32),
        in_specs=[vmem] * 4,
        out_specs=vmem,
        scratch_shapes=[
            pltpu.VMEM((m, *kv.shape), jnp.bfloat16),
            pltpu.VMEM((n, *bias.shape), jnp.bfloat16),
            pltpu.VMEM((m, *mask.shape), jnp.float32),
            pltpu.VMEM((heads * sites, m * sites), jnp.float32),
            pltpu.VMEM((lines, m * sites), jnp.float32),
            dma((3, parts)), dma((3, parts)),
            dma((n - 1,)), dma((n - 1,)), dma((m - 1,)), dma((m - 1,)),
        ],
        compiler_params=pltpu.CompilerParams(
            collective_id=2, has_side_effects=True, vmem_limit_bytes=32 * 1024 * 1024
        ),
        cost_estimate=pl.CostEstimate(
            flops=4 * lines * heads * sites * m * sites * width,
            bytes_accessed=4 << 20,
            transcendentals=lines * heads * sites * m * sites,
        ),
        name="attention",
    )(query, kv, bias, mask)


def factor_kernel(
    left, right, left_all, right_all, left_got, right_got,
    left_send, left_recv, right_send, right_recv,
):
    tiles = lax.axis_size("tile")
    n = left_got.shape[0]
    dap = lax.axis_index("dap")
    block = lax.axis_index("branch") * tiles + lax.axis_index("tile")

    def at(index, column):
        return {"branch": index // tiles, "tile": lax.rem(index, tiles), "dap": column}

    def others(index, column):
        return jnp.logical_or(index != block, column != dap)

    barrier = pltpu.get_barrier_semaphore()
    for k in range(1, n * n):
        peer = lax.rem(block * n + dap + k, n * n)
        pl.semaphore_signal(
            barrier, inc=1, device_id=at(peer // n, lax.rem(peer, n)), device_id_type=MESH
        )
    pl.semaphore_wait(barrier, n * n - 1)

    copies = [
        start_remote(
            left, left_got.at[dap], left_send.at[k - 1], left_recv.at[k - 1],
            {"dap": lax.rem(dap + k, n)},
        )
        for k in range(1, n)
    ]

    def right_copy(slot, index, column, k):
        return pltpu.make_async_remote_copy(
            src_ref=right,
            dst_ref=right_got.at[slot],
            send_sem=right_send.at[k],
            recv_sem=right_recv.at[slot],
            device_id=at(index, column),
            device_id_type=MESH,
        )

    for k in range(n):

        @pl.when(others(k, block))
        def _(k=k):
            right_copy(dap, k, block, k).start()

    left_got[dap] = left[...]

    @pl.when(dap == block)
    def _():
        right_got[dap] = right[...]

    for copy in copies:
        copy.wait()
    for k in range(n):

        @pl.when(others(dap, k))
        def _(k=k):
            right_copy(k, dap, k, k).wait_recv()

        @pl.when(others(k, block))
        def _(k=k):
            right_copy(dap, k, block, k).wait_send()

    left_all[...] = left_got[...]
    right_all[...] = right_got[...]


def trade_factors(left, right):
    n = lax.axis_size("dap")
    vmem = pl.BlockSpec(memory_space=pltpu.VMEM)
    dma = pltpu.SemaphoreType.DMA
    shape = (n, *left.shape)
    return pl.pallas_call(
        factor_kernel,
        out_shape=[jax.ShapeDtypeStruct(shape, jnp.bfloat16)] * 2,
        in_specs=[vmem] * 2,
        out_specs=[vmem] * 2,
        scratch_shapes=[
            pltpu.VMEM(shape, jnp.bfloat16),
            pltpu.VMEM(shape, jnp.bfloat16),
            dma((n - 1,)), dma((n - 1,)), dma((n,)), dma((n,)),
        ],
        compiler_params=pltpu.CompilerParams(collective_id=3, has_side_effects=True),
        cost_estimate=pl.CostEstimate(flops=0, bytes_accessed=1 << 20, transcendentals=0),
        name="factors",
    )(left, right)


def body(
    homolog_hidden,
    duo_hidden,
    homolog_valid_flags,
    duo_valid_flags,
    polymer_labeling,
    monomer_serials,
    separation_bin_vectors,
    duo_logit_rescale,
    duo_logit_projector,
    homolog_heeded_rescale,
    qkv_valve_projectors,
    heeded_exit_projector,
    dyadic_rescale,
    dyadic_factor_projector,
    dyadic_exit_projector,
    triad_entry_rescales,
    triad_entry_projectors,
    triad_valve_projectors,
    triad_exit_rescales,
    triad_exit_projectors,
):
    lines_each_shard, sites_each_shard, lineup_feature_extent = homolog_hidden.shape
    columns_per_device = duo_hidden.shape[1]
    number_of_heads = duo_logit_projector.shape[1]
    square = (
        duo_hidden.shape[:2] == (LANES // 2, LANES // 2)
        and lax.axis_size("branch") == lax.axis_size("tile") == 2
        and lax.axis_size("dap") == 4
    )
    head_channels = lineup_feature_extent // number_of_heads
    outer_channels = dyadic_factor_projector.shape[1] // 2
    row_start = lax.axis_index(("branch", "tile")) * sites_each_shard
    col_start = lax.axis_index("dap") * columns_per_device
    rel_reach = (REL_BINS - 2) // 2
    res_rows = lax.dynamic_slice_in_dim(monomer_serials, row_start, sites_each_shard)
    res_cols = lax.dynamic_slice_in_dim(monomer_serials, col_start, columns_per_device)
    chain_rows = lax.dynamic_slice_in_dim(polymer_labeling, row_start, sites_each_shard)
    chain_cols = lax.dynamic_slice_in_dim(polymer_labeling, col_start, columns_per_device)
    offset = jnp.clip(res_rows[:, None] - res_cols[None, :], -rel_reach, rel_reach) + rel_reach
    rel_bins = jnp.where(chain_rows[:, None] == chain_cols[None, :], offset, REL_BINS - 1)
    one_hot = (rel_bins[:, :, None] == jnp.arange(REL_BINS, dtype=jnp.int32)[None, None, :]).astype(
        jnp.bfloat16
    )
    duo_hidden_values = duo_hidden.astype(jnp.float32) + jnp.einsum(
        "ijb,bc->ijc", one_hot, separation_bin_vectors, preferred_element_type=jnp.float32
    )
    pair_normed = standardize_features(duo_hidden_values, duo_logit_rescale, 2).astype(jnp.bfloat16)
    lineup_standardized = standardize_features(homolog_hidden, homolog_heeded_rescale, 2).astype(
        jnp.bfloat16
    )
    mapped_contents = jnp.einsum(
        "ezp,pb->ezb", lineup_standardized, qkv_valve_projectors, preferred_element_type=jnp.float32
    )
    asking_array = (mapped_contents[..., :lineup_feature_extent] * head_channels ** (-0.5)).astype(
        jnp.bfloat16
    )
    asking_array = asking_array.reshape(
        lines_each_shard, sites_each_shard, number_of_heads, head_channels
    )
    key_value_pairs = mapped_contents[
        ..., lineup_feature_extent : 3 * lineup_feature_extent
    ].astype(jnp.bfloat16)
    sigmoid_switches = jax.nn.sigmoid(mapped_contents[..., 3 * lineup_feature_extent :])
    if square:
        pairs = sites_each_shard // 2
        pair_order = pair_normed.reshape(2, pairs, columns_per_device, -1).transpose(1, 0, 2, 3)
        local_bias = jnp.einsum(
            "tpc,ch->htp",
            pair_order.reshape(pairs, LANES, -1),
            duo_logit_projector,
            preferred_element_type=jnp.float32,
        ).astype(jnp.bfloat16)
        focused_readout = fused_attention(
            asking_array.reshape(homolog_hidden.shape),
            key_value_pairs,
            local_bias,
            jnp.pad(
                homolog_valid_flags.astype(jnp.float32), ((0, 0), (0, LANES - sites_each_shard))
            ),
            number_of_heads,
        )
    else:
        local_bias = jnp.einsum(
            "ijc,ch->hij", pair_normed, duo_logit_projector, preferred_element_type=jnp.float32
        ).astype(jnp.bfloat16)
        row_bias = lax.all_gather(
            local_bias.reshape(number_of_heads, sites_each_shard * columns_per_device), "dap", axis=0
        ).reshape(-1, number_of_heads, sites_each_shard, columns_per_device)
        row_bias = jnp.transpose(row_bias, (1, 2, 0, 3)).reshape(number_of_heads, sites_each_shard, -1)
        mask_grid = lax.all_gather(
            homolog_valid_flags.astype(jnp.bfloat16), ("dap", "branch", "tile"), axis=0
        ).reshape(lax.axis_size("dap"), -1, lines_each_shard, sites_each_shard)
        mask_grid = jnp.transpose(mask_grid, (0, 2, 1, 3)).reshape(
            lax.axis_size("dap") * lines_each_shard, -1
        )
        run_max = jnp.full((lines_each_shard, number_of_heads, sites_each_shard), -jnp.inf, jnp.float32)
        run_sum = jnp.zeros((lines_each_shard, number_of_heads, sites_each_shard), jnp.float32)
        run_acc = jnp.zeros(
            (lines_each_shard, number_of_heads, sites_each_shard, head_channels), jnp.float32
        )
        key_value_slice = lax.all_gather(key_value_pairs, ("branch", "tile"), axis=1, tiled=True)
        mask_piece = lax.dynamic_slice_in_dim(
            mask_grid, lax.axis_index("dap") * lines_each_shard, lines_each_shard, axis=0
        )
        slice_length = key_value_slice.shape[1]
        key_per_head = key_value_slice[..., :lineup_feature_extent].reshape(
            lines_each_shard, slice_length, number_of_heads, head_channels
        )
        value_per_head = key_value_slice[..., lineup_feature_extent:].reshape(
            lines_each_shard, slice_length, number_of_heads, head_channels
        )
        key_bias = row_bias.astype(jnp.float32)
        scores = jnp.einsum(
            "sihd,sjhd->shij", asking_array, key_per_head, preferred_element_type=jnp.float32
        )
        scores = (
            scores
            + key_bias[None]
            + ((mask_piece.astype(jnp.float32) - 1.0) * mask_big)[:, None, None, :]
        )
        new_max = jnp.max(scores, axis=-1)
        old_scale = jnp.exp(run_max - new_max)
        weights = jnp.exp(scores - new_max[..., None])
        run_sum = run_sum * old_scale + jnp.sum(weights, axis=-1)
        run_acc = run_acc * old_scale[..., None] + jnp.einsum(
            "shij,sjhd->shid",
            weights.astype(jnp.bfloat16),
            value_per_head,
            preferred_element_type=jnp.float32,
        )
        run_max, run_sum, run_acc = (new_max, run_sum, run_acc)
        focused_readout = run_acc / run_sum[..., None]
        focused_readout = jnp.transpose(focused_readout, (0, 2, 1, 3)).reshape(
            lines_each_shard, sites_each_shard, lineup_feature_extent
        )
    merged_focus_groups = (sigmoid_switches * focused_readout).astype(jnp.bfloat16)
    lineup_updated_state = (
        homolog_hidden.astype(jnp.float32)
        + jnp.einsum(
            "ezp,pb->ezb",
            merged_focus_groups,
            heeded_exit_projector,
            preferred_element_type=jnp.float32,
        )
    ).astype(jnp.bfloat16)
    outer_product_normalized = standardize_features(lineup_updated_state, dyadic_rescale, 2).astype(
        jnp.bfloat16
    )
    exit_by_channel = dyadic_exit_projector.reshape(outer_channels, outer_channels, -1)
    if square:
        flag_row = homolog_valid_flags.reshape(1, -1).astype(jnp.float32)
        factors = (
            jnp.einsum(
                "ep,pb->be",
                outer_product_normalized.reshape(-1, lineup_feature_extent),
                dyadic_factor_projector,
                preferred_element_type=jnp.float32,
            )
            * flag_row
        ).astype(jnp.bfloat16)
        flag_rows = jnp.broadcast_to(flag_row, (16, flag_row.shape[1])).astype(jnp.bfloat16)
        traded = trade_factors(
            jnp.concatenate([factors[:outer_channels], flag_rows]),
            jnp.concatenate([factors[outer_channels:], flag_rows]),
        )
        left_rows, right_rows = (
            part[:, :outer_channels]
            .reshape(-1, outer_channels, lines_each_shard, sites_each_shard)
            .transpose(0, 2, 3, 1)
            .reshape(-1, sites_each_shard, outer_channels)
            for part in traded
        )
        mask_rows, mask_right = (
            part[:, outer_channels].reshape(-1, sites_each_shard) for part in traded
        )
        counts = jnp.einsum("si,sj->ij", mask_rows, mask_right, preferred_element_type=jnp.float32)
        spread_right = jnp.einsum(
            "sjd,cdz->scjz", right_rows, exit_by_channel, preferred_element_type=jnp.float32
        ).astype(jnp.bfloat16)
        update = jnp.einsum(
            "sic,scjz->ijz", left_rows, spread_right, preferred_element_type=jnp.float32
        )
    else:
        factors = (
            jnp.einsum(
                "ezp,pb->ezb",
                outer_product_normalized,
                dyadic_factor_projector,
                preferred_element_type=jnp.float32,
            )
            * homolog_valid_flags.astype(jnp.float32)[..., None]
        )
        factors = factors.astype(jnp.bfloat16)
        all_factors = lax.all_gather(factors, ("dap", "branch", "tile"), axis=0).reshape(
            lax.axis_size("dap"), -1, lines_each_shard, sites_each_shard, 2 * outer_channels
        )
        alignment_rows = mask_grid.shape[0]
        left_rows = lax.dynamic_index_in_dim(
            all_factors, lax.axis_index(("branch", "tile")), axis=1, keepdims=False
        )[..., :outer_channels].reshape(alignment_rows, sites_each_shard, outer_channels)
        block = col_start // sites_each_shard
        right_rows = lax.dynamic_index_in_dim(all_factors, block, axis=1, keepdims=False)[
            ..., outer_channels:
        ].reshape(alignment_rows, sites_each_shard, outer_channels)
        right_rows = lax.dynamic_slice_in_dim(
            right_rows, col_start - block * sites_each_shard, columns_per_device, axis=1
        )
        mask_rows = lax.dynamic_slice_in_dim(mask_grid, row_start, sites_each_shard, axis=1)
        mask_right = lax.dynamic_slice_in_dim(mask_grid, col_start, columns_per_device, axis=1)
        counts = jnp.einsum("si,sj->ij", mask_rows, mask_right, preferred_element_type=jnp.float32)
        spread_right = jnp.einsum(
            "sjd,cdz->scjz", right_rows, exit_by_channel, preferred_element_type=jnp.float32
        ).astype(jnp.bfloat16)
        update = jnp.einsum(
            "sic,scjz->ijz", left_rows, spread_right, preferred_element_type=jnp.float32
        )
    duo_hidden_values = duo_hidden_values + update / (count_eps + counts)[..., None]
    for threefold_module in range(2):
        parameters = (
            triad_entry_rescales[threefold_module],
            triad_entry_projectors[threefold_module],
            triad_valve_projectors[threefold_module],
            triad_exit_rescales[threefold_module],
            triad_exit_projectors[threefold_module],
            threefold_module == 1,
        )
        if square:
            out_type = jnp.bfloat16 if threefold_module == 1 else jnp.float32
            duo_hidden_values = fused_update(
                duo_hidden_values, duo_valid_flags, *parameters, out_type
            )
        else:
            duo_hidden_values = threeway_update(duo_hidden_values, duo_valid_flags, *parameters)
    return (lineup_updated_state, duo_hidden_values.astype(jnp.bfloat16))


def solution(mesh):
    placed = (
        P(("groups", "dap"), ("branch", "tile"), None),
        P(("groups", "branch", "tile"), "dap", None),
        P(("groups", "dap"), ("branch", "tile")),
        P(("groups", "branch", "tile"), "dap"),
        P("groups"),
        P("groups"),
        P(),
        P(),
        P(),
        P(),
        P(),
        P(),
        P(),
        P(),
        P(),
        P(),
        P(),
        P(),
        P(),
        P(),
    )
    return jax.shard_map(
        body,
        mesh=mesh,
        in_specs=placed,
        out_specs=(
            P(("groups", "dap"), ("branch", "tile"), None),
            P(("groups", "branch", "tile"), "dap", None),
        ),
        check_vma=False,
    )
```

```python
import functools

import jax
import jax.numpy as jnp
from jax import lax
from jax.experimental import pallas as pl
from jax.experimental.pallas import tpu as pltpu
from jax.sharding import PartitionSpec as P

REL_BINS = 66


norm_eps = 1e-05
mask_big = 1000000000.0
count_eps = 0.001


def standardize_features(values, norm_gain, norm_axis):
    values = values.astype(jnp.float32)
    mean_val = jnp.mean(values, axis=norm_axis, keepdims=True)
    centred = values - mean_val
    spread = jnp.mean(centred * centred, axis=norm_axis, keepdims=True)
    return centred * lax.rsqrt(spread + norm_eps) * norm_gain


def threeway_update(
    duo_hidden_values, duo_valid_flags, norm_gain, w_in, w_gate, out_gain, w_out, incoming
):
    width_tri = w_in.shape[1] // 4
    rows, cols = duo_valid_flags.shape
    tri_normed = standardize_features(duo_hidden_values, norm_gain, 2).astype(jnp.bfloat16)
    flags = duo_valid_flags.astype(jnp.float32)
    if incoming:
        positions = jnp.transpose(tri_normed, (1, 0, 2))
        flags = flags.T
        share_axis, spread_axis = ("branch", "tile"), "dap"
        kept, summed = cols, rows
    else:
        positions = tri_normed
        share_axis, spread_axis = "dap", ("branch", "tile")
        kept, summed = rows, cols
    positions = positions.reshape(kept * summed, width_tri)
    flags = flags.reshape(1, kept * summed)
    shares = lax.axis_size(share_axis)
    share = width_tri // shares
    mapped = jnp.einsum("pc,cd->dp", positions, w_in, preferred_element_type=jnp.float32)
    blocks = [mapped[n * width_tri : (n + 1) * width_tri] for n in range(4)]
    left_fac = (jax.nn.sigmoid(blocks[1]) * blocks[0] * flags).astype(jnp.bfloat16)
    right_fac = (jax.nn.sigmoid(blocks[3]) * blocks[2] * flags).astype(jnp.bfloat16)

    def by_channel_share(factor):
        got = lax.all_to_all(
            factor.reshape(shares, share, kept * summed), share_axis, split_axis=0, concat_axis=0
        )
        got = got.reshape(shares, share, kept, summed)
        return jnp.transpose(got, (1, 2, 0, 3)).reshape(share, kept, shares * summed)

    if incoming:
        left_own = by_channel_share(left_fac)
        left_all = lax.all_gather(left_own, spread_axis, axis=0)
        right_own = by_channel_share(right_fac)
        product = jnp.einsum(
            "gcik,cjk->gicj", left_all, right_own, preferred_element_type=jnp.float32
        ).astype(jnp.bfloat16)
        product = product.reshape(shares, rows, share, cols)
        product = jnp.transpose(product, (0, 2, 1, 3))
    else:
        right_own = by_channel_share(right_fac)
        right_all = lax.all_gather(right_own, spread_axis, axis=0)
        left_own = by_channel_share(left_fac)
        product = jnp.einsum(
            "cik,gcjk->gjci", left_own, right_all, preferred_element_type=jnp.float32
        ).astype(jnp.bfloat16)
        product = product.reshape(shares, cols, share, rows)
        product = jnp.transpose(product, (0, 2, 3, 1))
    merged = lax.all_to_all(
        product.reshape(shares, share, rows * cols), share_axis, split_axis=0, concat_axis=0
    ).reshape(width_tri, rows * cols)
    sigmoid_switches = jax.nn.sigmoid(
        jnp.einsum("ijc,cd->ijd", tri_normed, w_gate, preferred_element_type=jnp.float32)
    )
    product_normed = standardize_features(merged, out_gain[:, None], 0).astype(jnp.bfloat16)
    update = jnp.einsum("cp,cz->pz", product_normed, w_out, preferred_element_type=jnp.float32)
    return duo_hidden_values + sigmoid_switches * update.reshape(rows, cols, width_tri)


MESH = pl.DeviceIdType.MESH
LANES = 128


def start_remote(src, dst, send_sem, recv_sem, device):
    copy = pltpu.make_async_remote_copy(
        src_ref=src,
        dst_ref=dst,
        send_sem=send_sem,
        recv_sem=recv_sem,
        device_id=device,
        device_id_type=MESH,
    )
    copy.start()
    return copy


def triangle_kernel(
    incoming,
    state,
    flags,
    norm_gain,
    w_own,
    w_spread,
    w_gate,
    out_gain,
    w_out,
    out,
    own_in,
    spread_in,
    normed,
    own,
    spread,
    own_wide,
    spread_wide,
    product_wide,
    outgoing_blocks,
    merged,
    trade_send,
    trade_recv,
    local_sem,
    spread_send,
    spread_recv,
    back_send,
    back_recv,
):
    n, pairs, share = own.shape[0], own.shape[1], own.shape[2]
    m = spread.shape[0]
    half = LANES // 2
    tiles = lax.axis_size("tile")
    branch, tile, dap = lax.axis_index("branch"), lax.axis_index("tile"), lax.axis_index("dap")
    block = branch * tiles + tile

    def by_block(index):
        return {"branch": index // tiles, "tile": lax.rem(index, tiles)}

    def by_dap(index):
        return {"dap": index}

    if incoming:
        me, trade_to, place, spread_to = block, by_block, dap, by_dap
    else:
        me, trade_to, place, spread_to = dap, by_dap, block, by_block

    barrier = pltpu.get_barrier_semaphore()
    for k in range(1, n):
        pl.semaphore_signal(
            barrier, inc=1, device_id=trade_to(lax.rem(me + k, n)), device_id_type=MESH
        )
    for k in range(1, m):
        pl.semaphore_signal(
            barrier, inc=1, device_id=spread_to(lax.rem(place + k, m)), device_id_type=MESH
        )
    rows, cols, width = state.shape

    def normalise(i, _):
        values = state[i]
        centred = values - jnp.mean(values, axis=1, keepdims=True)
        spread_of = jnp.mean(centred * centred, axis=1, keepdims=True)
        normed[pl.ds(pl.multiple_of(i * cols, cols), cols), :] = (
            centred * lax.rsqrt(spread_of + norm_eps) * norm_gain[...]
        )
        return 0

    lax.fori_loop(0, rows, normalise, 0, unroll=4)

    def project(weights, factor):
        def step(t, _):
            if incoming:
                chosen = [normed[pl.ds(t + part * pairs, rows, stride=cols), :] for part in (0, 1)]
            else:
                chosen = [
                    normed[pl.ds(pl.multiple_of((t + part * pairs) * cols, cols), cols), :]
                    for part in (0, 1)
                ]
            mapped = lax.dot_general(
                weights[...],
                jnp.concatenate(chosen, axis=0).astype(jnp.bfloat16),
                (((1,), (1,)), ((), ())),
                preferred_element_type=jnp.float32,
            )
            factor[t] = (jax.nn.sigmoid(mapped[width:]) * mapped[:width] * flags[t]).astype(
                jnp.bfloat16
            )
            return 0

        lax.fori_loop(0, pairs, step, 0, unroll=2)

    def channels(ref, index):
        return ref.at[:, pl.ds(pl.multiple_of(index * share, share), share), :]

    trades = [[], []]
    plans = ((w_spread, spread_in, spread.at[place, me]), (w_own, own_in, own.at[me]))
    for which, (weights, src, dst) in enumerate(plans):
        project(weights, src)
        if which == 0:
            pl.semaphore_wait(barrier, n + m - 2)
        for k in range(1, n):
            to = lax.rem(me + k, n)
            trades[which].append(
                start_remote(
                    channels(src, to),
                    dst,
                    trade_send.at[which, k - 1],
                    trade_recv.at[which, k - 1],
                    trade_to(to),
                )
            )
    locals_ = [
        pltpu.make_async_copy(channels(spread_in, me), spread.at[place, me], local_sem.at[0]),
        pltpu.make_async_copy(channels(own_in, me), own.at[me], local_sem.at[1]),
    ]
    for copy in locals_:
        copy.start()

    def widen(dst, load):
        def step(s, _):
            dst[pl.ds(pl.multiple_of(s * pairs * share, share), pairs * share), :] = (
                load(s).astype(jnp.float32).reshape(pairs * share, LANES)
            )
            return 0

        lax.fori_loop(0, n, step, 0)

    def matrix(ref, c):
        lower = lax.broadcasted_iota(jnp.int32, (pairs, LANES), 1) < half
        columns = []
        for s in range(0, n, 2):
            first = ref[pl.ds(s * pairs * share + c, pairs, stride=share), :]
            second = ref[pl.ds((s + 1) * pairs * share + c, pairs, stride=share), :]
            top = jnp.where(lower, first, pltpu.roll(second, half, 1))
            bottom = jnp.where(lower, pltpu.roll(first, half, 1), second)
            columns.append(jnp.concatenate([top, bottom], axis=0))
        return jnp.concatenate(columns, axis=1).astype(jnp.bfloat16)

    def multiply(g):
        widen(spread_wide, lambda s: spread[g, s])

        def step(c, _):
            mine, other = matrix(own_wide, c), matrix(spread_wide, c)
            left, right = (other, mine) if incoming else (mine, other)
            found = lax.dot_general(
                left, right, (((1,), (1,)), ((), ())), preferred_element_type=jnp.float32
            )
            product_wide[pl.ds(c, pairs, stride=share), :] = jnp.concatenate(
                [found[:pairs], found[pairs:]], axis=1
            )
            return 0

        lax.fori_loop(0, share, step, 0, unroll=8)
        outgoing_blocks[g] = (
            product_wide[...].reshape(pairs, share, LANES).astype(jnp.bfloat16)
        )

        @pl.when(g != me)
        def _():
            start_remote(
                outgoing_blocks.at[g],
                merged.at[me],
                back_send.at[g],
                back_recv.at[me],
                trade_to(g),
            )

        @pl.when(g == me)
        def _():
            merged[g] = outgoing_blocks[g]

    def spread_copy(g, k, slot, device):
        piece = spread.at[g, lax.rem(me - k + n, n)]
        return pltpu.make_async_remote_copy(
            src_ref=piece,
            dst_ref=piece,
            send_sem=spread_send.at[slot, k],
            recv_sem=spread_recv.at[slot, k],
            device_id=device,
            device_id_type=MESH,
        )

    def turn_to_gate(i, _):
        here = pl.ds(pl.multiple_of(i * cols, cols), cols)
        normed[here, :] = jax.nn.sigmoid(
            jnp.dot(
                normed[here, :].astype(jnp.bfloat16),
                w_gate[...],
                preferred_element_type=jnp.float32,
            )
        )
        return 0

    def finish_own():
        lax.fori_loop(0, rows, turn_to_gate, 0, unroll=4)
        locals_[1].wait()
        for copy in trades[1]:
            copy.wait()
        widen(own_wide, lambda s: own[s])

    if incoming:
        right, left = place + 1, place - 1
        has_right, has_left = right < m, left >= 0
        sides = ((0, 1, right, has_right), (1, -1, left, has_left))
        for k in range(n):
            if k == 0:
                locals_[0].wait()
            else:
                trades[0][k - 1].wait()
            for side, _, to, there in sides:

                @pl.when(there)
                def _(side=side, to=to, k=k):
                    spread_copy(place, k, side * (m - 1), spread_to(to)).start()

        finish_own()
        multiply(place)
        for h in range(1, m):
            for k in range(n):
                for side, sign, to, there in sides:
                    g = place - sign * h
                    has_block = (g >= 0) if sign > 0 else (g < m)

                    @pl.when(has_block)
                    def _(side=side, to=to, there=there, g=g, h=h, k=k):
                        spread_copy(
                            g, k, side * (m - 1) + h - 1, spread_to(lax.rem(place + 1, m))
                        ).wait_recv()
                        if h < m - 1:

                            @pl.when(there)
                            def _():
                                spread_copy(g, k, side * (m - 1) + h, spread_to(to)).start()

            for side, sign, to, there in sides:
                g = place - sign * h
                has_block = (g >= 0) if sign > 0 else (g < m)

                @pl.when(has_block)
                def _(g=g):
                    multiply(g)

        for side, sign, to, there in sides:
            for h in range(m - 1):
                g = place - sign * h
                has_block = (g >= 0) if sign > 0 else (g < m)

                @pl.when(jnp.logical_and(there, has_block))
                def _(side=side, g=g, h=h, to=to):
                    for k in range(n):
                        spread_copy(g, k, side * (m - 1) + h, spread_to(to)).wait_send()

    else:
        across = (1 - branch) * tiles + tile
        beside = branch * tiles + (1 - tile)
        beyond = (1 - branch) * tiles + (1 - tile)
        to_tile, to_branch = spread_to(beside), spread_to(across)
        copies = []
        for k in range(n):
            if k == 0:
                locals_[0].wait()
            else:
                trades[0][k - 1].wait()
            for slot, device in ((0, to_tile), (1, to_branch)):
                copy = spread_copy(place, k, slot, device)
                copy.start()
                copies.append(copy)
        finish_own()
        for k in range(n):
            spread_copy(beside, k, 0, to_tile).wait_recv()
            copy = spread_copy(beside, k, 2, to_branch)
            copy.start()
            copies.append(copy)
        multiply(place)
        multiply(beside)
        for k in range(n):
            spread_copy(across, k, 1, to_branch).wait_recv()
        multiply(across)
        for k in range(n):
            spread_copy(beyond, k, 2, to_branch).wait_recv()
        multiply(beyond)
        for copy in copies:
            copy.wait_send()

    for k in range(1, n):
        source = lax.rem(me - k + n, n)
        pltpu.make_async_remote_copy(
            src_ref=outgoing_blocks.at[source],
            dst_ref=merged.at[source],
            send_sem=back_send.at[source],
            recv_sem=back_recv.at[source],
            device_id=trade_to(source),
            device_id_type=MESH,
        ).wait()

    def finish(t, _):
        found = merged[:, pl.ds(t, 1)].astype(jnp.float32).reshape(n * share, LANES)
        centred = found - jnp.mean(found, axis=0, keepdims=True)
        spread_of = jnp.mean(centred * centred, axis=0, keepdims=True)
        scaled = (centred * lax.rsqrt(spread_of + norm_eps) * out_gain[...]).astype(jnp.bfloat16)
        update = lax.dot_general(
            scaled, w_out[...], (((0,), (0,)), ((), ())), preferred_element_type=jnp.float32
        )
        for part in range(2):
            i = part * pairs + t
            gate = normed[pl.ds(pl.multiple_of(i * cols, cols), cols), :]
            out[i] = (state[i] + gate * update[part * half : (part + 1) * half]).astype(out.dtype)
        return 0

    lax.fori_loop(0, pairs, finish, 0, unroll=4)


def fused_update(
    state, flags, norm_gain, w_in, w_gate, out_gain, w_out, incoming, out_type
):
    width = w_in.shape[1] // 4
    rows, cols = flags.shape
    n = lax.axis_size("dap")
    share, pairs = width // n, rows // 2
    flags = flags.astype(jnp.float32)
    flags = (flags.T if incoming else flags).reshape(2, pairs, -1)
    flags = flags.transpose(1, 0, 2).reshape(pairs, 1, LANES)
    turned = w_in.T
    left, right = turned[: 2 * width], turned[2 * width :]
    own, spread = (right, left) if incoming else (left, right)
    slots = 2 * (n - 1)
    vmem = pl.BlockSpec(memory_space=pltpu.VMEM)
    factor = (n, pairs, share, LANES)
    return pl.pallas_call(
        functools.partial(triangle_kernel, incoming),
        out_shape=jax.ShapeDtypeStruct(state.shape, out_type),
        in_specs=[vmem] * 8,
        out_specs=vmem,
        scratch_shapes=[
            pltpu.VMEM((pairs, width, LANES), jnp.bfloat16),
            pltpu.VMEM((pairs, width, LANES), jnp.bfloat16),
            pltpu.VMEM((rows * cols, width), jnp.float32),
            pltpu.VMEM(factor, jnp.bfloat16),
            pltpu.VMEM((n, *factor), jnp.bfloat16),
            pltpu.VMEM((n * pairs * share, LANES), jnp.float32),
            pltpu.VMEM((n * pairs * share, LANES), jnp.float32),
            pltpu.VMEM((pairs * share, LANES), jnp.float32),
            pltpu.VMEM(factor, jnp.bfloat16),
            pltpu.VMEM(factor, jnp.bfloat16),
            pltpu.SemaphoreType.DMA((2, n - 1)),
            pltpu.SemaphoreType.DMA((2, n - 1)),
            pltpu.SemaphoreType.DMA((2,)),
            pltpu.SemaphoreType.DMA((slots, n)),
            pltpu.SemaphoreType.DMA((slots, n)),
            pltpu.SemaphoreType.DMA((n,)),
            pltpu.SemaphoreType.DMA((n,)),
        ],
        compiler_params=pltpu.CompilerParams(
            collective_id=1 if incoming else 0,
            has_side_effects=True,
            vmem_limit_bytes=40 * 1024 * 1024,
        ),
        cost_estimate=pl.CostEstimate(
            flops=2 * 256 * rows * cols * width, bytes_accessed=8 << 20, transcendentals=0
        ),
        name="triangle_in" if incoming else "triangle_out",
    )(
        state,
        flags,
        norm_gain.reshape(1, width),
        own,
        spread,
        w_gate,
        out_gain.reshape(width, 1),
        w_out,
    )


def attention_kernel(
    heads, query, own_kv, own_bias, own_mask, out, kv, bias, mask, bias_wide, mask_wide,
    kv_send, kv_recv, bias_send, bias_recv, mask_send, mask_recv,
):
    tiles = lax.axis_size("tile")
    n, m = bias.shape[0], kv.shape[0]
    lines, sites, width = query.shape
    half = LANES // 2
    branch, tile, dap = lax.axis_index("branch"), lax.axis_index("tile"), lax.axis_index("dap")
    place = branch * tiles + tile

    def at(index):
        return {"branch": index // tiles, "tile": lax.rem(index, tiles)}

    barrier = pltpu.get_barrier_semaphore()
    for k in range(1, n):
        pl.semaphore_signal(
            barrier, inc=1, device_id={"dap": lax.rem(dap + k, n)}, device_id_type=MESH
        )
    for k in range(1, m):
        pl.semaphore_signal(
            barrier, inc=1, device_id=at(lax.rem(place + k, m)), device_id_type=MESH
        )
    pl.semaphore_wait(barrier, n + m - 2)

    across = (1 - branch) * tiles + tile
    beside = branch * tiles + (1 - tile)
    beyond = (1 - branch) * tiles + (1 - tile)
    to_tile, to_branch = at(beside), at(across)
    parts = kv_send.shape[1]
    step_lines = lines // parts

    def kv_copy(g, q, slot, device, src=None):
        piece = kv.at[g, pl.ds(q * step_lines, step_lines)]
        return pltpu.make_async_remote_copy(
            src_ref=piece if src is None else src.at[pl.ds(q * step_lines, step_lines)],
            dst_ref=piece,
            send_sem=kv_send.at[slot, q],
            recv_sem=kv_recv.at[slot, q],
            device_id=device,
            device_id_type=MESH,
        )

    waits = []
    for q in range(parts):
        for slot, device in ((0, to_tile), (1, to_branch)):
            copy = kv_copy(place, q, slot, device, own_kv)
            copy.start()
            waits.append(copy)
    small = []
    for k in range(1, m):
        small.append(
            start_remote(
                own_mask, mask.at[place], mask_send.at[k - 1], mask_recv.at[k - 1],
                at(lax.rem(place + k, m)),
            )
        )
    for k in range(1, n):
        small.append(
            start_remote(
                own_bias, bias.at[dap], bias_send.at[k - 1], bias_recv.at[k - 1],
                {"dap": lax.rem(dap + k, n)},
            )
        )
    kv[place] = own_kv[...]
    bias[dap] = own_bias[...]
    mask[place] = own_mask[...]
    for copy in small:
        copy.wait()

    for g in range(0, m, 2):
        lower = lax.broadcasted_iota(jnp.int32, (lines, LANES), 1) < half
        both = jnp.where(lower, mask[g], pltpu.roll(mask[g + 1], half, 1))
        mask_wide[:, (g // 2) * LANES : (g // 2 + 1) * LANES] = (both - 1.0) * mask_big
    for g in range(0, n, 2):
        for h in range(heads):
            first = bias[g, h].astype(jnp.float32)
            second = bias[g + 1, h].astype(jnp.float32)
            lower = lax.broadcasted_iota(jnp.int32, first.shape, 1) < half
            top = jnp.where(lower, first, pltpu.roll(second, half, 1))
            bottom = jnp.where(lower, pltpu.roll(first, half, 1), second)
            bias_wide[h * sites : (h + 1) * sites, (g // 2) * LANES : (g // 2 + 1) * LANES] = (
                jnp.concatenate([top, bottom], axis=0)
            )

    head_width = width // heads
    head_of = lax.broadcasted_iota(jnp.int32, (sites, width), 1) // head_width

    def attend(line):
        asked = query[line]
        stacked = jnp.concatenate(
            [jnp.where(head_of == h, asked, jnp.zeros_like(asked)) for h in range(heads)], axis=0
        )
        pairs = kv[:, line].reshape(m * sites, 2 * width)
        scores = lax.dot_general(
            stacked, pairs[:, :width], (((1,), (1,)), ((), ())), preferred_element_type=jnp.float32
        )
        scores = scores + bias_wide[...] + mask_wide[line : line + 1]
        weights = jnp.exp(scores - jnp.max(scores, axis=1, keepdims=True))
        row_sum = jnp.sum(weights, axis=1, keepdims=True)
        found = (
            jnp.dot(
                weights.astype(jnp.bfloat16), pairs[:, width:], preferred_element_type=jnp.float32
            )
            / row_sum
        )
        joined = jnp.zeros((sites, width), jnp.float32)
        for h in range(heads):
            joined = jnp.where(head_of == h, found[h * sites : (h + 1) * sites], joined)
        out[line] = joined

    def finish_part(q):
        kv_copy(across, q, 1, to_branch).wait_recv()
        kv_copy(beyond, q, 2, to_branch).wait_recv()
        for line in range(q * step_lines, (q + 1) * step_lines):
            attend(line)

    for q in range(parts):
        kv_copy(beside, q, 0, to_tile).wait_recv()
        copy = kv_copy(beside, q, 2, to_branch)
        copy.start()
        waits.append(copy)
        if q:
            finish_part(q - 1)
    finish_part(parts - 1)
    for copy in waits:
        copy.wait_send()


def fused_attention(query, kv, bias, mask, heads):
    lines, sites, width = query.shape
    n, m, parts = lax.axis_size("dap"), lax.axis_size(("branch", "tile")), 4
    vmem = pl.BlockSpec(memory_space=pltpu.VMEM)
    dma = pltpu.SemaphoreType.DMA
    return pl.pallas_call(
        functools.partial(attention_kernel, heads),
        out_shape=jax.ShapeDtypeStruct(query.shape, jnp.float32),
        in_specs=[vmem] * 4,
        out_specs=vmem,
        scratch_shapes=[
            pltpu.VMEM((m, *kv.shape), jnp.bfloat16),
            pltpu.VMEM((n, *bias.shape), jnp.bfloat16),
            pltpu.VMEM((m, *mask.shape), jnp.float32),
            pltpu.VMEM((heads * sites, m * sites), jnp.float32),
            pltpu.VMEM((lines, m * sites), jnp.float32),
            dma((3, parts)), dma((3, parts)),
            dma((n - 1,)), dma((n - 1,)), dma((m - 1,)), dma((m - 1,)),
        ],
        compiler_params=pltpu.CompilerParams(
            collective_id=2, has_side_effects=True, vmem_limit_bytes=32 * 1024 * 1024
        ),
        cost_estimate=pl.CostEstimate(
            flops=4 * lines * heads * sites * m * sites * width,
            bytes_accessed=4 << 20,
            transcendentals=lines * heads * sites * m * sites,
        ),
        name="attention",
    )(query, kv, bias, mask)


def factor_kernel(
    left, right, left_all, right_all, left_got, right_got,
    left_send, left_recv, right_send, right_recv,
):
    tiles = lax.axis_size("tile")
    n = left_got.shape[0]
    dap = lax.axis_index("dap")
    block = lax.axis_index("branch") * tiles + lax.axis_index("tile")

    def at(index, column):
        return {"branch": index // tiles, "tile": lax.rem(index, tiles), "dap": column}

    def others(index, column):
        return jnp.logical_or(index != block, column != dap)

    barrier = pltpu.get_barrier_semaphore()
    for k in range(1, n * n):
        peer = lax.rem(block * n + dap + k, n * n)
        pl.semaphore_signal(
            barrier, inc=1, device_id=at(peer // n, lax.rem(peer, n)), device_id_type=MESH
        )
    pl.semaphore_wait(barrier, n * n - 1)

    copies = [
        start_remote(
            left, left_got.at[dap], left_send.at[k - 1], left_recv.at[k - 1],
            {"dap": lax.rem(dap + k, n)},
        )
        for k in range(1, n)
    ]

    def right_copy(slot, index, column, k):
        return pltpu.make_async_remote_copy(
            src_ref=right,
            dst_ref=right_got.at[slot],
            send_sem=right_send.at[k],
            recv_sem=right_recv.at[slot],
            device_id=at(index, column),
            device_id_type=MESH,
        )

    for k in range(n):

        @pl.when(others(k, block))
        def _(k=k):
            right_copy(dap, k, block, k).start()

    left_got[dap] = left[...]

    @pl.when(dap == block)
    def _():
        right_got[dap] = right[...]

    for copy in copies:
        copy.wait()
    for k in range(n):

        @pl.when(others(dap, k))
        def _(k=k):
            right_copy(k, dap, k, k).wait_recv()

        @pl.when(others(k, block))
        def _(k=k):
            right_copy(dap, k, block, k).wait_send()

    left_all[...] = left_got[...]
    right_all[...] = right_got[...]


def trade_factors(left, right):
    n = lax.axis_size("dap")
    vmem = pl.BlockSpec(memory_space=pltpu.VMEM)
    dma = pltpu.SemaphoreType.DMA
    shape = (n, *left.shape)
    return pl.pallas_call(
        factor_kernel,
        out_shape=[jax.ShapeDtypeStruct(shape, jnp.bfloat16)] * 2,
        in_specs=[vmem] * 2,
        out_specs=[vmem] * 2,
        scratch_shapes=[
            pltpu.VMEM(shape, jnp.bfloat16),
            pltpu.VMEM(shape, jnp.bfloat16),
            dma((n - 1,)), dma((n - 1,)), dma((n,)), dma((n,)),
        ],
        compiler_params=pltpu.CompilerParams(collective_id=3, has_side_effects=True),
        cost_estimate=pl.CostEstimate(flops=0, bytes_accessed=1 << 20, transcendentals=0),
        name="factors",
    )(left, right)


def body(
    homolog_hidden,
    duo_hidden,
    homolog_valid_flags,
    duo_valid_flags,
    polymer_labeling,
    monomer_serials,
    separation_bin_vectors,
    duo_logit_rescale,
    duo_logit_projector,
    homolog_heeded_rescale,
    qkv_valve_projectors,
    heeded_exit_projector,
    dyadic_rescale,
    dyadic_factor_projector,
    dyadic_exit_projector,
    triad_entry_rescales,
    triad_entry_projectors,
    triad_valve_projectors,
    triad_exit_rescales,
    triad_exit_projectors,
):
    lines_each_shard, sites_each_shard, lineup_feature_extent = homolog_hidden.shape
    columns_per_device = duo_hidden.shape[1]
    number_of_heads = duo_logit_projector.shape[1]
    square = (
        duo_hidden.shape[:2] == (LANES // 2, LANES // 2)
        and lax.axis_size("branch") == lax.axis_size("tile") == 2
        and lax.axis_size("dap") == 4
    )
    head_channels = lineup_feature_extent // number_of_heads
    outer_channels = dyadic_factor_projector.shape[1] // 2
    row_start = lax.axis_index(("branch", "tile")) * sites_each_shard
    col_start = lax.axis_index("dap") * columns_per_device
    rel_reach = (REL_BINS - 2) // 2
    res_rows = lax.dynamic_slice_in_dim(monomer_serials, row_start, sites_each_shard)
    res_cols = lax.dynamic_slice_in_dim(monomer_serials, col_start, columns_per_device)
    chain_rows = lax.dynamic_slice_in_dim(polymer_labeling, row_start, sites_each_shard)
    chain_cols = lax.dynamic_slice_in_dim(polymer_labeling, col_start, columns_per_device)
    offset = jnp.clip(res_rows[:, None] - res_cols[None, :], -rel_reach, rel_reach) + rel_reach
    rel_bins = jnp.where(chain_rows[:, None] == chain_cols[None, :], offset, REL_BINS - 1)
    one_hot = (rel_bins[:, :, None] == jnp.arange(REL_BINS, dtype=jnp.int32)[None, None, :]).astype(
        jnp.bfloat16
    )
    duo_hidden_values = duo_hidden.astype(jnp.float32) + jnp.einsum(
        "ijb,bc->ijc", one_hot, separation_bin_vectors, preferred_element_type=jnp.float32
    )
    pair_normed = standardize_features(duo_hidden_values, duo_logit_rescale, 2).astype(jnp.bfloat16)
    lineup_standardized = standardize_features(homolog_hidden, homolog_heeded_rescale, 2).astype(
        jnp.bfloat16
    )
    mapped_contents = jnp.einsum(
        "ezp,pb->ezb", lineup_standardized, qkv_valve_projectors, preferred_element_type=jnp.float32
    )
    asking_array = (mapped_contents[..., :lineup_feature_extent] * head_channels ** (-0.5)).astype(
        jnp.bfloat16
    )
    asking_array = asking_array.reshape(
        lines_each_shard, sites_each_shard, number_of_heads, head_channels
    )
    key_value_pairs = mapped_contents[
        ..., lineup_feature_extent : 3 * lineup_feature_extent
    ].astype(jnp.bfloat16)
    sigmoid_switches = jax.nn.sigmoid(mapped_contents[..., 3 * lineup_feature_extent :])
    if square:
        pairs = sites_each_shard // 2
        pair_order = pair_normed.reshape(2, pairs, columns_per_device, -1).transpose(1, 0, 2, 3)
        local_bias = jnp.einsum(
            "tpc,ch->htp",
            pair_order.reshape(pairs, LANES, -1),
            duo_logit_projector,
            preferred_element_type=jnp.float32,
        ).astype(jnp.bfloat16)
        focused_readout = fused_attention(
            asking_array.reshape(homolog_hidden.shape),
            key_value_pairs,
            local_bias,
            jnp.pad(
                homolog_valid_flags.astype(jnp.float32), ((0, 0), (0, LANES - sites_each_shard))
            ),
            number_of_heads,
        )
    else:
        local_bias = jnp.einsum(
            "ijc,ch->hij", pair_normed, duo_logit_projector, preferred_element_type=jnp.float32
        ).astype(jnp.bfloat16)
        row_bias = lax.all_gather(
            local_bias.reshape(number_of_heads, sites_each_shard * columns_per_device), "dap", axis=0
        ).reshape(-1, number_of_heads, sites_each_shard, columns_per_device)
        row_bias = jnp.transpose(row_bias, (1, 2, 0, 3)).reshape(number_of_heads, sites_each_shard, -1)
        mask_grid = lax.all_gather(
            homolog_valid_flags.astype(jnp.bfloat16), ("dap", "branch", "tile"), axis=0
        ).reshape(lax.axis_size("dap"), -1, lines_each_shard, sites_each_shard)
        mask_grid = jnp.transpose(mask_grid, (0, 2, 1, 3)).reshape(
            lax.axis_size("dap") * lines_each_shard, -1
        )
        run_max = jnp.full((lines_each_shard, number_of_heads, sites_each_shard), -jnp.inf, jnp.float32)
        run_sum = jnp.zeros((lines_each_shard, number_of_heads, sites_each_shard), jnp.float32)
        run_acc = jnp.zeros(
            (lines_each_shard, number_of_heads, sites_each_shard, head_channels), jnp.float32
        )
        key_value_slice = lax.all_gather(key_value_pairs, ("branch", "tile"), axis=1, tiled=True)
        mask_piece = lax.dynamic_slice_in_dim(
            mask_grid, lax.axis_index("dap") * lines_each_shard, lines_each_shard, axis=0
        )
        slice_length = key_value_slice.shape[1]
        key_per_head = key_value_slice[..., :lineup_feature_extent].reshape(
            lines_each_shard, slice_length, number_of_heads, head_channels
        )
        value_per_head = key_value_slice[..., lineup_feature_extent:].reshape(
            lines_each_shard, slice_length, number_of_heads, head_channels
        )
        key_bias = row_bias.astype(jnp.float32)
        scores = jnp.einsum(
            "sihd,sjhd->shij", asking_array, key_per_head, preferred_element_type=jnp.float32
        )
        scores = (
            scores
            + key_bias[None]
            + ((mask_piece.astype(jnp.float32) - 1.0) * mask_big)[:, None, None, :]
        )
        new_max = jnp.max(scores, axis=-1)
        old_scale = jnp.exp(run_max - new_max)
        weights = jnp.exp(scores - new_max[..., None])
        run_sum = run_sum * old_scale + jnp.sum(weights, axis=-1)
        run_acc = run_acc * old_scale[..., None] + jnp.einsum(
            "shij,sjhd->shid",
            weights.astype(jnp.bfloat16),
            value_per_head,
            preferred_element_type=jnp.float32,
        )
        run_max, run_sum, run_acc = (new_max, run_sum, run_acc)
        focused_readout = run_acc / run_sum[..., None]
        focused_readout = jnp.transpose(focused_readout, (0, 2, 1, 3)).reshape(
            lines_each_shard, sites_each_shard, lineup_feature_extent
        )
    merged_focus_groups = (sigmoid_switches * focused_readout).astype(jnp.bfloat16)
    lineup_updated_state = (
        homolog_hidden.astype(jnp.float32)
        + jnp.einsum(
            "ezp,pb->ezb",
            merged_focus_groups,
            heeded_exit_projector,
            preferred_element_type=jnp.float32,
        )
    ).astype(jnp.bfloat16)
    outer_product_normalized = standardize_features(lineup_updated_state, dyadic_rescale, 2).astype(
        jnp.bfloat16
    )
    exit_by_channel = dyadic_exit_projector.reshape(outer_channels, outer_channels, -1)
    if square:
        flag_row = homolog_valid_flags.reshape(1, -1).astype(jnp.float32)
        factors = (
            jnp.einsum(
                "ep,pb->be",
                outer_product_normalized.reshape(-1, lineup_feature_extent),
                dyadic_factor_projector,
                preferred_element_type=jnp.float32,
            )
            * flag_row
        ).astype(jnp.bfloat16)
        flag_rows = jnp.broadcast_to(flag_row, (16, flag_row.shape[1])).astype(jnp.bfloat16)
        traded = trade_factors(
            jnp.concatenate([factors[:outer_channels], flag_rows]),
            jnp.concatenate([factors[outer_channels:], flag_rows]),
        )
        left_rows, right_rows = (
            part[:, :outer_channels]
            .reshape(-1, outer_channels, lines_each_shard, sites_each_shard)
            .transpose(0, 2, 3, 1)
            .reshape(-1, sites_each_shard, outer_channels)
            for part in traded
        )
        mask_rows, mask_right = (
            part[:, outer_channels].reshape(-1, sites_each_shard) for part in traded
        )
        counts = jnp.einsum("si,sj->ij", mask_rows, mask_right, preferred_element_type=jnp.float32)
        spread_right = jnp.einsum(
            "sjd,cdz->scjz", right_rows, exit_by_channel, preferred_element_type=jnp.float32
        ).astype(jnp.bfloat16)
        update = jnp.einsum(
            "sic,scjz->ijz", left_rows, spread_right, preferred_element_type=jnp.float32
        )
    else:
        factors = (
            jnp.einsum(
                "ezp,pb->ezb",
                outer_product_normalized,
                dyadic_factor_projector,
                preferred_element_type=jnp.float32,
            )
            * homolog_valid_flags.astype(jnp.float32)[..., None]
        )
        factors = factors.astype(jnp.bfloat16)
        all_factors = lax.all_gather(factors, ("dap", "branch", "tile"), axis=0).reshape(
            lax.axis_size("dap"), -1, lines_each_shard, sites_each_shard, 2 * outer_channels
        )
        alignment_rows = mask_grid.shape[0]
        left_rows = lax.dynamic_index_in_dim(
            all_factors, lax.axis_index(("branch", "tile")), axis=1, keepdims=False
        )[..., :outer_channels].reshape(alignment_rows, sites_each_shard, outer_channels)
        block = col_start // sites_each_shard
        right_rows = lax.dynamic_index_in_dim(all_factors, block, axis=1, keepdims=False)[
            ..., outer_channels:
        ].reshape(alignment_rows, sites_each_shard, outer_channels)
        right_rows = lax.dynamic_slice_in_dim(
            right_rows, col_start - block * sites_each_shard, columns_per_device, axis=1
        )
        mask_rows = lax.dynamic_slice_in_dim(mask_grid, row_start, sites_each_shard, axis=1)
        mask_right = lax.dynamic_slice_in_dim(mask_grid, col_start, columns_per_device, axis=1)
        counts = jnp.einsum("si,sj->ij", mask_rows, mask_right, preferred_element_type=jnp.float32)
        spread_right = jnp.einsum(
            "sjd,cdz->scjz", right_rows, exit_by_channel, preferred_element_type=jnp.float32
        ).astype(jnp.bfloat16)
        update = jnp.einsum(
            "sic,scjz->ijz", left_rows, spread_right, preferred_element_type=jnp.float32
        )
    duo_hidden_values = duo_hidden_values + update / (count_eps + counts)[..., None]
    for threefold_module in range(2):
        parameters = (
            triad_entry_rescales[threefold_module],
            triad_entry_projectors[threefold_module],
            triad_valve_projectors[threefold_module],
            triad_exit_rescales[threefold_module],
            triad_exit_projectors[threefold_module],
            threefold_module == 1,
        )
        if square:
            out_type = jnp.bfloat16 if threefold_module == 1 else jnp.float32
            duo_hidden_values = fused_update(
                duo_hidden_values, duo_valid_flags, *parameters, out_type
            )
        else:
            duo_hidden_values = threeway_update(duo_hidden_values, duo_valid_flags, *parameters)
    return (lineup_updated_state, duo_hidden_values.astype(jnp.bfloat16))


def solution(mesh):
    placed = (
        P(("groups", "dap"), ("branch", "tile"), None),
        P(("groups", "branch", "tile"), "dap", None),
        P(("groups", "dap"), ("branch", "tile")),
        P(("groups", "branch", "tile"), "dap"),
        P("groups"),
        P("groups"),
        P(),
        P(),
        P(),
        P(),
        P(),
        P(),
        P(),
        P(),
        P(),
        P(),
        P(),
        P(),
        P(),
        P(),
    )
    return jax.shard_map(
        body,
        mesh=mesh,
        in_specs=placed,
        out_specs=(
            P(("groups", "dap"), ("branch", "tile"), None),
            P(("groups", "branch", "tile"), "dap", None),
        ),
        check_vma=False,
    )
```
